256 devices in a mesh: fsdp: 32 (over x_hi, z, core), tp: 8 (over x_lo, y).
Axes of the slice: x: 4 (x_hi: 2, x_lo: 2; x = x_hi * 2 + x_lo), y: 4, z: 8, core: 2. Of those that a mesh axis runs over, the one named last changes fastest.
Arguments:
- q_weight: bfloat16 [8192, 8192], P(('tp', 'fsdp')), may hold values from -6 to 6
- k_weight: bfloat16 [8192, 1024], P(('tp', 'fsdp')), may hold values from -6 to 6
- v_weight: bfloat16 [8192, 1024], P(('tp', 'fsdp')), may hold values from -6 to 6
- gate_weight: bfloat16 [8192, 28672], P(('tp', 'fsdp')), may hold values from -6 to 6
- up_weight: bfloat16 [8192, 28672], P(('tp', 'fsdp')), may hold values from -6 to 6
- down_weight: bfloat16 [28672, 8192], P(('tp', 'fsdp')), may hold values from -6 to 6
- attn_gain: float32 [8192], P(('tp', 'fsdp')), may hold values from 0.5 to 2
- ffn_gain: float32 [8192], P(('tp', 'fsdp')), may hold values from 0.5 to 2
- head_order: int32 [8, 8], replicated, may hold values from 0 to 7, each once within a row
- ffn_order: int32 [8, 28], replicated, may hold values from 0 to 27, each once within a row
Outputs:
- merged_qkv: bfloat16 [8192, 10240], P('fsdp', 'tp')
- merged_gate_up: bfloat16 [8192, 57344], P('fsdp', 'tp')
- merged_down: bfloat16 [28672, 8192], P('tp', 'fsdp')
The draws below stay inside these ranges and needn't reach their ends.
Inputs may be any that keep to these rules, and one draw needn't show every extreme that they name: `head_order`: each row is a permutation of 0 to 7. `ffn_order`: each row is a permutation of 0 to 27.
All inputs are finite; a program needn't handle non-finite values.
Results may differ from the reference program's by a relative error of at most 0.0058.
Values may be sent and summed in bfloat16 or wider, within the bound.
No kernel may reach another device: no remote copies, remote signals or barrier semaphores. Data moves between devices by JAX's collectives and lax.ppermute only.
A program may use at most 128 MiB of HBM per device.

```python
import math
import jax
import jax.numpy as jnp
from jax import lax

D = 8192
FF = 28672
QH = 64
KV = 8
HD = 128
HA = 64
FB = 128
HB = 128
QPG = 8
FFB = 28
N_TP = 8


def levels(key, shape, cuts, smallest, top_value):
    loudness, own = 1.0, jax.random.fold_in(key, 6)
    for position, blocks in cuts:
        draws = jnp.exp(jax.random.uniform(jax.random.fold_in(own, position), (blocks,), jnp.float32, smallest / len(cuts), top_value / len(cuts)))
        loudness = loudness * jnp.repeat(draws, shape[position] // blocks).reshape([-1 if axis == position else 1 for axis in range(len(shape))])
    return loudness


def gaussian(rng, extent, scale, bound, cuts=(), kind=jnp.bfloat16):
    loudness = levels(rng, extent, cuts, -0.22, 0.18) if cuts else 1.0
    array = jax.random.normal(rng, extent, jnp.float32) * scale * loudness
    return jnp.minimum(jnp.maximum(array, -bound), bound).astype(kind)


def setup_inputs(seed: int = 0) -> dict:
    seeds = jax.random.split(jax.random.key(seed), 11)
    q_weight = gaussian(seeds[0], (D, QH * HD), 1.0, 6.0, ((0, 256),))
    k_weight = gaussian(seeds[1], (D, KV * HD), 1.0, 6.0, ((0, 256),))
    v_weight = gaussian(seeds[2], (D, KV * HD), 1.0, 6.0, ((0, 256),))
    gate_weight = gaussian(seeds[3], (D, FF), 1.0, 6.0, ((0, 256),))
    up_weight = gaussian(seeds[4], (D, FF), 1.0, 6.0, ((0, 256),))
    down_weight = gaussian(seeds[5], (FF, D), 1.0, 6.0, ((0, 256),))
    attn_gain = jnp.clip(jnp.exp(math.log(2.0) - 1.3862944 * jax.random.uniform(seeds[6], (D,), jnp.float32) ** levels(seeds[6], (D,), ((0, 256),), -0.2, 0.2)), 0.5, 2.0)
    ffn_gain = jnp.clip(jnp.exp(math.log(2.0) - 1.3862944 * jax.random.uniform(seeds[7], (D,), jnp.float32) ** levels(seeds[7], (D,), ((0, 256),), -0.2, 0.2)), 0.5, 2.0)
    head_order = jax.vmap(lambda own: jax.random.permutation(own, QPG))(jax.random.split(seeds[8], KV)).reshape((KV, QPG)).astype(jnp.int32)
    ffn_order = jax.vmap(lambda own: jax.random.permutation(own, FFB))(jax.random.split(seeds[9], N_TP)).reshape((N_TP, FFB)).astype(jnp.int32)
    return {"q_weight": q_weight, "k_weight": k_weight, "v_weight": v_weight, "gate_weight": gate_weight, "up_weight": up_weight, "down_weight": down_weight, "attn_gain": attn_gain, "ffn_gain": ffn_gain, "head_order": head_order, "ffn_order": ffn_order}


def sylvester(order_size):
    counter = jnp.arange(order_size, dtype=jnp.int32)
    parity = jnp.zeros((order_size, order_size), jnp.int32)
    for bit_level in range(order_size.bit_length() - 1):
        digits = counter // 2 ** bit_level % 2
        parity = parity + digits[:, None] * digits[None, :]
    return (1 - 2 * (parity % 2)).astype(jnp.bfloat16)

def qkv_index(head_order, owners):
    group_per = KV // owners
    owner_ids = jnp.arange(owners, dtype=jnp.int32)[:, None]
    head_local = jnp.arange(group_per * QPG, dtype=jnp.int32)[None, :]
    groups = owner_ids * group_per + head_local // QPG
    slots = head_local % QPG
    heads = groups * QPG + head_order.reshape(-1)[groups * QPG + slots]
    within = jnp.arange(HD, dtype=jnp.int32)
    query_cols = (heads[:, :, None] * HD + within).reshape(owners, -1)
    kv_groups = owner_ids * group_per + jnp.arange(group_per, dtype=jnp.int32)[None, :]
    key_cols = (QH * HD + kv_groups[:, :, None] * HD + within).reshape(owners, -1)
    value_cols = ((QH + KV) * HD + kv_groups[:, :, None] * HD + within).reshape(owners, -1)
    return jnp.concatenate([query_cols, key_cols, value_cols], axis=1).reshape(-1).astype(jnp.int32)

def ffn_units(ffn_order, owners):
    per_owner = FF // owners
    owner_ids = jnp.arange(owners, dtype=jnp.int32)[:, None]
    inside = (ffn_order[:, :, None] * FB + jnp.arange(FB, dtype=jnp.int32)[None, None, :]).reshape(owners, per_owner)
    return (owner_ids * per_owner + inside).astype(jnp.int32)

def ffn_index(ffn_order, owners):
    units = ffn_units(ffn_order, owners)
    return jnp.concatenate([units, FF + units], axis=1).reshape(-1).astype(jnp.int32)

def scale_rows(matrix, gain):
    return (gain[:, None] * matrix.astype(jnp.float32)).astype(jnp.bfloat16)

def first_factor(matrix, large_sign):
    column_count = matrix.shape[-1]
    shaped = matrix.reshape(-1, large_sign.shape[0], column_count).astype(jnp.float32)
    mixed = jnp.einsum('bc,acw->abw', large_sign.astype(jnp.float32), shaped, precision=lax.Precision.HIGHEST)
    return (mixed * (1.0 / math.sqrt(large_sign.shape[0]))).reshape(matrix.shape).astype(jnp.bfloat16)

def second_factor(matrix, small_sign):
    shaped = matrix.reshape(small_sign.shape[0], -1).astype(jnp.float32)
    mixed = jnp.dot(small_sign.astype(jnp.float32), shaped, precision=lax.Precision.HIGHEST)
    return (mixed * (1.0 / math.sqrt(small_sign.shape[0]))).reshape(matrix.shape).astype(jnp.bfloat16)

def rotate_columns(matrix, small_sign, large_sign):
    row_count = matrix.shape[0]
    shaped = matrix.reshape(row_count, small_sign.shape[0], large_sign.shape[0]).astype(jnp.float32)
    sectioned = jnp.einsum('rab,bc->rac', shaped, large_sign.astype(jnp.float32), precision=lax.Precision.HIGHEST)
    sectioned = (sectioned * (1.0 / math.sqrt(large_sign.shape[0]))).astype(jnp.bfloat16)
    mixed = jnp.einsum('rac,ae->rec', sectioned.astype(jnp.float32), small_sign.astype(jnp.float32), precision=lax.Precision.HIGHEST)
    return (mixed * (1.0 / math.sqrt(small_sign.shape[0]))).reshape(matrix.shape).astype(jnp.bfloat16)

def rotate_wide(matrix, gain, small_sign, large_sign):
    column_count = matrix.shape[1]
    part_width = min(512, column_count)
    pieces = matrix.reshape(D, column_count // part_width, part_width).transpose(1, 0, 2)

    def one_part(piece):
        return second_factor(first_factor(scale_rows(piece, gain), large_sign), small_sign)
    rotated = lax.map(one_part, pieces)
    return rotated.transpose(1, 0, 2).reshape(D, column_count)

def reference(q_weight, k_weight, v_weight, gate_weight, up_weight, down_weight, attn_gain, ffn_gain, head_order, ffn_order):
    small_sign = sylvester(HA)
    large_sign = sylvester(HB)
    attn_source = jnp.take(jnp.concatenate([q_weight, k_weight, v_weight], axis=1), qkv_index(head_order, N_TP), axis=1)
    merged_qkv = rotate_wide(attn_source, attn_gain, small_sign, large_sign)
    ffn_source = jnp.take(jnp.concatenate([gate_weight, up_weight], axis=1), ffn_index(ffn_order, N_TP), axis=1)
    merged_gate_up = rotate_wide(ffn_source, ffn_gain, small_sign, large_sign)
    down_rows = jnp.take(down_weight, ffn_units(ffn_order, N_TP).reshape(-1), axis=0)
    part_rows = min(512, FF)
    down_pieces = down_rows.reshape(FF // part_rows, part_rows, D)
    merged_down = lax.map(lambda piece: rotate_columns(piece, small_sign, large_sign), down_pieces).reshape(FF, D)
    return (merged_qkv, merged_gate_up, merged_down)
```

```python
import functools
import math

import jax
import jax.numpy as jnp
import numpy as np
from jax import lax
from jax.experimental import pallas as pl
from jax.experimental.pallas import tpu as pltpu
from jax.sharding import Mesh
from jax.sharding import PartitionSpec as P

BLK = 128
QPG = 8
FFB = 28
HALF_Q = QPG // 2
HALF_F = FFB // 2
ROWS = 32
PIECES = 16
VMEM_LIMIT = 48 * 1024 * 1024
PLANE = ("xh", "xl", "y")
DEPTH = ("xh", "z")
FSDP = ("xh", "z", "core")
TP = ("xl", "y")


def signs(order):
    index = np.arange(order)
    common = index[:, None] & index[None, :]
    parity = np.zeros((order, order), np.int64)
    while common.any():
        parity ^= common & 1
        common = common >> 1
    return (1 - 2 * parity).astype(np.float32)


def first_matrix():
    high = signs(PIECES)[:, [(s & 7) * 2 + (s >> 3) for s in range(PIECES)]]
    return np.kron(high, signs(ROWS)) / 16.0


def last_matrices():
    table = np.zeros((2, 2, 8, 8), np.float32)
    for core in range(2):
        for side in range(2):
            b5 = core ^ side
            for row in range(8):
                for col in range(8):
                    bits = (core & (col >> 2)) + ((row >> 2) & (col >> 1)) % 2
                    bits += ((row >> 1) & col) % 2 + (row & 1 & b5)
                    table[core, side, row, col] = 1 - 2 * (bits % 2)
    return np.kron(table, np.eye(ROWS, dtype=np.float32).reshape(1, 1, ROWS, ROWS))


def bf16(values):
    return values.astype(jnp.bfloat16)


def params():
    return pltpu.CompilerParams(vmem_limit_bytes=VMEM_LIMIT)


def cost(flops, moved):
    return pl.CostEstimate(flops=int(flops), bytes_accessed=int(moved), transcendentals=0)


def whole(count):
    return [pl.BlockSpec(memory_space=pltpu.VMEM)] * count


def down_kernel(weight_ref, sign_ref, out_ref):
    sign = sign_ref[...]
    groups = weight_ref.shape[1] // BLK

    @pl.loop(0, weight_ref.shape[0] // 16)
    def _(step):
        rows = pl.ds(pl.multiple_of(step * 16, 16), 16)
        tall = jnp.concatenate(
            [weight_ref[rows, a * BLK : (a + 1) * BLK] for a in range(groups)], axis=0
        )
        half = jnp.dot(tall, sign, preferred_element_type=jnp.float32)
        half = bf16(half * (1.0 / math.sqrt(BLK))).astype(jnp.float32)
        parts = [half[a * 16 : (a + 1) * 16] for a in range(groups)]
        span = 1
        while span < groups:
            mixed = list(parts)
            for a in range(groups):
                if not a & span:
                    mixed[a] = parts[a] + parts[a | span]
                    mixed[a | span] = parts[a] - parts[a | span]
            parts = mixed
            span *= 2
        for a in range(groups):
            value = bf16(parts[a] * (1.0 / math.sqrt(groups)))
            out_ref[a // 2, rows, (a % 2) * BLK : (a % 2 + 1) * BLK] = value


def rotate_down(weight, shards):
    rows, width = weight.shape
    return pl.pallas_call(
        down_kernel,
        out_shape=jax.ShapeDtypeStruct((shards, rows, width // shards), jnp.bfloat16),
        in_specs=whole(2),
        out_specs=whole(1)[0],
        compiler_params=params(),
        cost_estimate=cost(2 * rows * width * BLK * 4, 4 * rows * width),
        name="down_rotate",
    )(weight, jnp.asarray(signs(BLK), jnp.bfloat16))


def scaled(ref, block, gain):
    columns = pl.ds(pl.multiple_of(block * BLK, BLK), BLK)
    return bf16(ref[:, columns].astype(jnp.float32) * gain)


def pick_kernel(with_heads, place_ref, heads_ref, order_ref, gain_ref, *refs):
    out_refs = refs[-PIECES:]
    place = place_ref[0]
    ffn_ref = refs[0]
    ffn_gain = gain_ref[0]

    @pl.loop(0, HALF_F)
    def _(slot):
        columns = pl.ds(pl.multiple_of(slot * BLK, BLK), BLK)
        for k in range(PIECES):
            place_to = place ^ k
            owner = place_to & 7
            block = order_ref[owner, (place_to >> 3) * HALF_F + slot]
            out_refs[k][:, columns] = scaled(ffn_ref, owner * FFB + block, ffn_gain)

    if with_heads:
        q_ref, k_ref, v_ref = refs[1:4]
        head_gain = gain_ref[1]
        start = HALF_F * BLK

        @pl.loop(0, HALF_Q)
        def _(slot):
            columns = pl.ds(pl.multiple_of(start + slot * BLK, BLK), BLK)
            for k in range(PIECES):
                place_to = place ^ k
                owner = place_to & 7
                head = heads_ref[owner, (place_to >> 3) * HALF_Q + slot]
                out_refs[k][:, columns] = scaled(q_ref, owner * QPG + head, head_gain)

        for k in range(PIECES):
            place_to = place ^ k
            owner = place_to & 7
            value = jnp.where(
                place_to >= 8, scaled(v_ref, owner, head_gain), scaled(k_ref, owner, head_gain)
            )
            out_refs[k][:, start + HALF_Q * BLK :] = value


def pick(place, head_order, ffn_order, gains, arrays):
    with_heads = len(arrays) > 1
    width = (HALF_F + (HALF_Q + 1) * with_heads) * BLK
    return pl.pallas_call(
        functools.partial(pick_kernel, with_heads),
        out_shape=[jax.ShapeDtypeStruct((ROWS, width), jnp.bfloat16)] * PIECES,
        in_specs=[pl.BlockSpec(memory_space=pltpu.SMEM)] * 3 + whole(1 + len(arrays)),
        out_specs=whole(PIECES),
        compiler_params=params(),
        cost_estimate=cost(PIECES * ROWS * width * 400, 4 * PIECES * ROWS * width),
        name="pick_columns",
    )(place, head_order, ffn_order, gains, *arrays)


def first_kernel(place_ref, matrix_ref, *refs):
    in_refs, (out_ref, mine_ref) = refs[:PIECES], refs[PIECES:]
    place = place_ref[0]
    for group in range(PIECES):
        turned = (group >> 1) | ((group & 1) << 3)
        common = place & turned
        common = common ^ (common >> 2)
        common = (common ^ (common >> 1)) & 1
        sign = bf16((1 - 2 * common).astype(jnp.float32))
        rows = slice(group * ROWS, (group + 1) * ROWS)
        mine_ref[rows, :] = matrix_ref[rows, :] * sign
    width = in_refs[0].shape[1]

    @pl.loop(0, width // BLK)
    def _(step):
        columns = pl.ds(pl.multiple_of(step * BLK, BLK), BLK)
        tall = jnp.concatenate([ref[:, columns] for ref in in_refs], axis=0)
        mixed = jnp.dot(mine_ref[...], tall, preferred_element_type=jnp.float32)
        out_ref[:, :, columns] = bf16(mixed).reshape(PIECES, ROWS, BLK)


def first_mix(place, pieces):
    width = pieces[0].shape[1]
    rows = PIECES * ROWS
    return pl.pallas_call(
        first_kernel,
        out_shape=jax.ShapeDtypeStruct((PIECES, ROWS, width), jnp.bfloat16),
        in_specs=[pl.BlockSpec(memory_space=pltpu.SMEM)] + whole(1 + PIECES),
        out_specs=whole(1)[0],
        scratch_shapes=[pltpu.VMEM((rows, rows), jnp.bfloat16)],
        compiler_params=params(),
        cost_estimate=cost(2 * rows * rows * width, 4 * rows * width),
        name="first_mix",
    )(place, jnp.asarray(first_matrix(), jnp.bfloat16), *pieces)


def last_columns(core_ref, matrix_ref, own_ref, other_ref, part, columns):
    core = core_ref[0]
    own = own_ref[pl.ds(part * 8, 8), :, columns].reshape(8 * ROWS, -1)
    other = other_ref[pl.ds(part * 8, 8), :, columns].reshape(8 * ROWS, -1)
    mixed = jnp.dot(matrix_ref[core, 0], own, preferred_element_type=jnp.float32)
    mixed += jnp.dot(matrix_ref[core, 1], other, preferred_element_type=jnp.float32)
    return bf16(mixed * (16.0 / math.sqrt(8192.0)))


def last_kernel(offset, with_heads, core_ref, matrix_ref, own_ref, other_ref, *refs):
    out_ref = refs[-1 - with_heads]
    part = pl.program_id(0)

    @pl.loop(0, HALF_F // 2)
    def _(step):
        columns = pl.ds(pl.multiple_of(step * 2 * BLK, 2 * BLK), 2 * BLK)
        out_ref[:, columns] = last_columns(
            core_ref, matrix_ref, own_ref, other_ref, part, columns
        )

    if with_heads:
        heads_ref = refs[-1]
        start = HALF_F * BLK
        middle = start + HALF_Q * BLK
        heads_ref[:, pl.ds(pl.multiple_of(part * HALF_Q * BLK, BLK), HALF_Q * BLK)] = last_columns(
            core_ref, matrix_ref, own_ref, other_ref, part, slice(start, middle)
        )
        heads_ref[:, pl.ds(pl.multiple_of((QPG + part) * BLK, BLK), BLK)] = last_columns(
            core_ref, matrix_ref, own_ref, other_ref, part, slice(middle, middle + BLK)
        )


def last_mix(core, own, other, offset, with_heads, target=None):
    width = own.shape[2]
    rows = 8 * ROWS
    outs = [jax.ShapeDtypeStruct((rows, 2 * FFB * BLK), jnp.bfloat16)]
    out_specs = [pl.BlockSpec((rows, HALF_F * BLK), lambda c: (0, offset + c))]
    if with_heads:
        outs.append(jax.ShapeDtypeStruct((rows, (QPG + 2) * BLK), jnp.bfloat16))
        out_specs.append(pl.BlockSpec((rows, (QPG + 2) * BLK), lambda c: (0, 0)))
    in_specs = [pl.BlockSpec(memory_space=pltpu.SMEM)] + whole(3)
    args = [core, jnp.asarray(last_matrices(), jnp.bfloat16), own, other]
    aliases = {}
    if target is not None:
        in_specs.append(pl.BlockSpec(memory_space=pl.ANY))
        args.append(target)
        aliases = {4: 0}
    return pl.pallas_call(
        functools.partial(last_kernel, offset, with_heads),
        grid=(2,),
        out_shape=outs,
        in_specs=in_specs,
        out_specs=out_specs,
        input_output_aliases=aliases,
        compiler_params=params(),
        cost_estimate=cost(8 * rows * rows * width, 12 * rows * width),
        name="last_mix",
    )(*args)


def order_kernel(owner_ref, order_ref, in_ref, out_ref):
    owner = owner_ref[0]
    for slot in range(FFB):
        block = order_ref[owner, slot]
        out_ref[slot * BLK : (slot + 1) * BLK, :] = in_ref[
            pl.ds(pl.multiple_of(block * BLK, BLK), BLK), :
        ]


def order_rows(owner, ffn_order, rows):
    return pl.pallas_call(
        order_kernel,
        out_shape=jax.ShapeDtypeStruct(rows.shape, jnp.bfloat16),
        in_specs=[pl.BlockSpec(memory_space=pltpu.SMEM)] * 2 + whole(1),
        out_specs=whole(1)[0],
        compiler_params=params(),
        cost_estimate=cost(rows.size, 4 * rows.size),
        name="order_rows",
    )(owner, ffn_order, rows)


def scalar(value):
    return value.astype(jnp.int32).reshape(1)


def exchange_plane(pieces):
    got = [pieces[0]]
    for k in range(1, PIECES):
        got.append(lax.ppermute(pieces[k], PLANE, [(i, i ^ k) for i in range(PIECES)]))
    return got


def exchange_depth(mixed):
    return lax.all_to_all(mixed, DEPTH, split_axis=0, concat_axis=0, tiled=True)


def exchange_core(got):
    return lax.ppermute(got, "core", [(0, 1), (1, 0)])


def per_device(
    q_weight,
    k_weight,
    v_weight,
    gate_weight,
    up_weight,
    down_weight,
    attn_gain,
    ffn_gain,
    head_order,
    ffn_order,
):
    shards = math.prod(lax.axis_size(name) for name in FSDP)
    owner = scalar(lax.axis_index(TP))
    place = scalar(lax.axis_index(PLANE))
    core = scalar(lax.axis_index("core"))
    gains = jnp.broadcast_to(jnp.stack([ffn_gain, attn_gain])[:, :, None], (2, ROWS, BLK))
    down_rotated = rotate_down(down_weight, shards)
    moved = lax.all_to_all(down_rotated, FSDP, split_axis=0, concat_axis=0, tiled=True)
    first = pick(place, head_order, ffn_order, gains, [gate_weight, q_weight, k_weight, v_weight])
    second = pick(place, head_order, ffn_order, gains, [up_weight])
    first_got = exchange_depth(first_mix(place, exchange_plane(first)))
    second_got = exchange_depth(first_mix(place, exchange_plane(second)))
    merged_ffn, merged_attn = last_mix(core, first_got, exchange_core(first_got), 0, True)
    (merged_ffn,) = last_mix(core, second_got, exchange_core(second_got), 2, False, merged_ffn)
    merged_down = order_rows(owner, ffn_order, moved.reshape(-1, moved.shape[2]))
    return (merged_attn, merged_ffn, merged_down)


def solution(mesh):
    split = Mesh(mesh.devices.reshape(2, 8, 2, 2, 4), ("xh", "z", "core", "xl", "y"))
    rows = TP + FSDP
    placed = (P(rows, None),) * 6 + (P(rows),) * 2 + (P(), P())
    return jax.shard_map(
        per_device,
        mesh=split,
        in_specs=placed,
        out_specs=(P(FSDP, TP), P(FSDP, TP), P(TP, FSDP)),
        check_vma=False,
    )
```

```python
import functools
import math

import jax
import jax.numpy as jnp
import numpy as np
from jax import lax
from jax.experimental import pallas as pl
from jax.experimental.pallas import tpu as pltpu
from jax.sharding import Mesh
from jax.sharding import PartitionSpec as P

BLK = 128
QPG = 8
FFB = 28
HALF_Q = QPG // 2
HALF_F = FFB // 2
ROWS = 32
PIECES = 16
DEEP = 8
Q_START = HALF_F * BLK
UP_START = Q_START + (HALF_Q + 1) * BLK
WIDTH = UP_START + HALF_F * BLK
VMEM_LIMIT = 16 * 1024 * 1024
VMEM_MOST = 56 * 1024 * 1024
PLANE = ("xh", "xl", "y")
DEPTH = ("xh", "z")
FSDP = ("xh", "z", "core")
TP = ("xl", "y")


def signs(order):
    index = np.arange(order)
    common = index[:, None] & index[None, :]
    parity = np.zeros((order, order), np.int64)
    while common.any():
        parity ^= common & 1
        common = common >> 1
    return (1 - 2 * parity).astype(np.float32)


def first_matrix():
    high = signs(PIECES)[:, [(s & 7) * 2 + (s >> 3) for s in range(PIECES)]]
    return np.kron(high, signs(ROWS)) / 16.0


def bf16(values):
    return values.astype(jnp.bfloat16)


def params(limit=VMEM_LIMIT):
    return pltpu.CompilerParams(vmem_limit_bytes=limit)


def cost(flops, moved):
    return pl.CostEstimate(flops=int(flops), bytes_accessed=int(moved), transcendentals=0)


def side_index():
    return lax.axis_index("xh") * 2 + lax.axis_index("core")


def whole(count):
    return [pl.BlockSpec(memory_space=pltpu.VMEM)] * count


def pair_sums(values, span):
    out = list(values)
    for i in range(len(values)):
        if not i & span:
            out[i] = values[i] + values[i | span]
            out[i | span] = values[i] - values[i | span]
    return out


def down_kernel(weight_ref, sign_ref, *refs):
    out_refs, held_ref = refs[:DEEP], refs[DEEP]
    sign = sign_ref[...]
    groups = weight_ref.shape[1] // BLK
    side, z = side_index(), lax.axis_index("z")

    @pl.loop(0, weight_ref.shape[0] // 16)
    def _(step):
        rows = pl.ds(pl.multiple_of(step * 16, 16), 16)
        tall = jnp.concatenate(
            [weight_ref[rows, a * BLK : (a + 1) * BLK] for a in range(groups)], axis=0
        )
        half = jnp.dot(tall, sign, preferred_element_type=jnp.float32)
        half = bf16(half * (1.0 / math.sqrt(BLK))).astype(jnp.float32)
        parts = [half[a * 16 : (a + 1) * 16] for a in range(groups)]
        span = 1
        while span < groups:
            parts = pair_sums(parts, span)
            span *= 2
        for a in range(groups):
            held_ref[a] = bf16(parts[a] * (1.0 / math.sqrt(groups)))
        for s in range(DEEP):
            for r in range(4):
                there = side ^ r
                shard = (there >> 1) * 2 * DEEP + ((z + s) & (DEEP - 1)) * 2 + (there & 1)
                for a in range(2):
                    out_refs[s][r, rows, a * BLK : (a + 1) * BLK] = held_ref[shard * 2 + a]


def rotate_down(weight, shards):
    rows, width = weight.shape
    groups = width // BLK
    return pl.pallas_call(
        down_kernel,
        out_shape=[jax.ShapeDtypeStruct((4, rows, width // shards), jnp.bfloat16)] * DEEP,
        in_specs=whole(2),
        out_specs=whole(DEEP),
        scratch_shapes=[pltpu.VMEM((groups, 16, BLK), jnp.bfloat16)],
        compiler_params=params(),
        cost_estimate=cost(2 * rows * width * BLK * 4, 4 * rows * width),
        name="down_rotate",
    )(weight, jnp.asarray(signs(BLK), jnp.bfloat16))


def repack_kernel(*refs):
    in_refs, out_refs = refs[:DEEP], refs[DEEP:]
    for r in range(4):
        for s in range(DEEP):
            out_refs[r][s] = in_refs[s][r]


def repack(pieces):
    _, rows, width = pieces[0].shape
    return pl.pallas_call(
        repack_kernel,
        out_shape=[jax.ShapeDtypeStruct((DEEP, rows, width), jnp.bfloat16)] * 4,
        in_specs=whole(DEEP),
        out_specs=whole(4),
        compiler_params=params(),
        cost_estimate=cost(4 * DEEP * rows * width, 16 * DEEP * rows * width),
        name="repack_down",
    )(*pieces)


def spread(gain_ref):
    row = lax.broadcasted_iota(jnp.int32, (ROWS, BLK), 0)
    spread_gain = jnp.zeros((ROWS, BLK), jnp.float32)
    for i in range(ROWS):
        spread_gain = jnp.where(row == i, gain_ref[i], spread_gain)
    return spread_gain


def scaled(ref, block, gain):
    columns = pl.ds(pl.multiple_of(block * BLK, BLK), BLK)
    return bf16(ref[:, columns].astype(jnp.float32) * gain)


def pick_kernel(
    heads_ref, order_ref, attn_ref, ffn_ref, q_ref, k_ref, v_ref, gate_ref, up_ref, out_ref
):
    ffn_gain, attn_gain = spread(ffn_ref), spread(attn_ref)
    each = out_ref.shape[0]
    for j in range(each):
        piece = pl.program_id(0) * each + j
        owner, half = piece & 7, piece >> 3
        for slot in range(HALF_F):
            block = owner * FFB + order_ref[owner, half * HALF_F + slot]
            for ref, start in ((gate_ref, 0), (up_ref, UP_START)):
                columns = slice(start + slot * BLK, start + (slot + 1) * BLK)
                out_ref[j, :, columns] = scaled(ref, block, ffn_gain)
        for slot in range(HALF_Q):
            head = owner * QPG + heads_ref[owner, half * HALF_Q + slot]
            columns = slice(Q_START + slot * BLK, Q_START + (slot + 1) * BLK)
            out_ref[j, :, columns] = scaled(q_ref, head, attn_gain)
        out_ref[j, :, UP_START - BLK : UP_START] = jnp.where(
            half == 1, scaled(v_ref, owner, attn_gain), scaled(k_ref, owner, attn_gain)
        )


def pick(head_order, ffn_order, gains, arrays):
    each = 4
    return pl.pallas_call(
        pick_kernel,
        grid=(PIECES // each,),
        out_shape=jax.ShapeDtypeStruct((PIECES, ROWS, WIDTH), jnp.bfloat16),
        in_specs=[pl.BlockSpec(memory_space=pltpu.SMEM)] * 4
        + [pl.BlockSpec(array.shape, lambda i: (0, 0)) for array in arrays],
        out_specs=pl.BlockSpec((each, ROWS, WIDTH), lambda i: (i, 0, 0)),
        compiler_params=params(VMEM_MOST),
        cost_estimate=cost(PIECES * ROWS * WIDTH * 400, 4 * PIECES * ROWS * WIDTH),
        name="pick_columns",
    )(head_order, ffn_order, *gains, *arrays)


def first_kernel(begin, matrix_ref, in_ref, out_ref):
    width = out_ref.shape[2]
    matrix = matrix_ref[...]
    for start in range(0, width, 2 * BLK):
        stop = min(start + 2 * BLK, width)
        tall = in_ref[:, :, begin + start : begin + stop].reshape(PIECES * ROWS, -1)
        mixed = jnp.dot(matrix, tall, preferred_element_type=jnp.float32)
        out_ref[:, :, start:stop] = bf16(mixed).reshape(-1, ROWS, stop - start)


def first_mix(pieces, begin, width):
    rows = PIECES * ROWS
    return pl.pallas_call(
        functools.partial(first_kernel, begin),
        grid=(2,),
        out_shape=jax.ShapeDtypeStruct((PIECES, ROWS, width), jnp.bfloat16),
        in_specs=[pl.BlockSpec((rows // 2, rows), lambda i: (i, 0))] + whole(1),
        out_specs=pl.BlockSpec((PIECES // 2, ROWS, width), lambda i: (i, 0, 0)),
        compiler_params=params(),
        cost_estimate=cost(2 * rows * rows * width, 4 * rows * width),
        name="first_mix",
    )(jnp.asarray(first_matrix(), jnp.bfloat16), pieces)


def last_columns(sign, own_ref, other_ref, part, columns):
    sides = []
    for ref in (own_ref, other_ref):
        rows = [ref[part * 8 + j, :, columns].astype(jnp.float32) for j in range(8)]
        rows = [rows[j] + sign * rows[j + 4] for j in range(4)]
        sides.append(pair_sums(pair_sums(rows, 2), 1))
    scale = 16.0 / math.sqrt(8192.0)
    parts = []
    for mine, theirs in zip(*sides):
        parts.append(bf16((mine + theirs) * scale))
        parts.append(bf16((mine - theirs) * (scale * sign)))
    return jnp.concatenate(parts, axis=0)


def last_kernel(with_heads, own_ref, other_ref, *refs):
    out_ref = refs[-1 - with_heads]
    part = pl.program_id(0)
    sign = (1 - 2 * lax.axis_index("core")).astype(jnp.float32)

    @pl.loop(0, HALF_F // 2)
    def _(step):
        columns = pl.ds(pl.multiple_of(step * 2 * BLK, 2 * BLK), 2 * BLK)
        out_ref[:, columns] = last_columns(sign, own_ref, other_ref, part, columns)

    if with_heads:
        heads_ref = refs[-1]
        start = HALF_F * BLK

        @pl.loop(0, HALF_Q + 1)
        def _(slot):
            columns = pl.ds(pl.multiple_of(start + slot * BLK, BLK), BLK)
            block = jnp.where(slot < HALF_Q, part * HALF_Q + slot, QPG + part)
            heads_ref[:, pl.ds(pl.multiple_of(block * BLK, BLK), BLK)] = last_columns(
                sign, own_ref, other_ref, part, columns
            )


def last_mix(own, other, offset, with_heads, target=None):
    width = own.shape[2]
    rows = 8 * ROWS
    outs = [jax.ShapeDtypeStruct((rows, 2 * FFB * BLK), jnp.bfloat16)]
    out_specs = [pl.BlockSpec((rows, HALF_F * BLK), lambda c: (0, offset + c))]
    if with_heads:
        outs.append(jax.ShapeDtypeStruct((rows, (QPG + 2) * BLK), jnp.bfloat16))
        out_specs.append(pl.BlockSpec((rows, (QPG + 2) * BLK), lambda c: (0, 0)))
    in_specs = whole(2)
    args = [own, other]
    aliases = {}
    if target is not None:
        in_specs.append(pl.BlockSpec(memory_space=pl.ANY))
        args.append(target)
        aliases = {2: 0}
    return pl.pallas_call(
        functools.partial(last_kernel, with_heads),
        grid=(2,),
        out_shape=outs,
        in_specs=in_specs,
        out_specs=out_specs,
        input_output_aliases=aliases,
        compiler_params=params(),
        cost_estimate=cost(40 * rows * width, 12 * rows * width),
        name="last_mix",
    )(*args)


def order_kernel(order_ref, *refs):
    in_refs, (out_ref, slot_ref) = refs[:4], refs[4:]
    owner = lax.axis_index("xl") * 4 + lax.axis_index("y")
    side, z = side_index(), lax.axis_index("z")
    for slot in range(FFB):
        slot_ref[order_ref[owner, slot]] = slot
    groups = in_refs[0].shape[1] // 16
    for r in range(4):
        there = side ^ r
        for s in range(DEEP):
            shard = (there >> 1) * 2 * DEEP + ((z - s) & (DEEP - 1)) * 2 + (there & 1)
            for group in range(groups):
                at = shard * groups + group
                row = slot_ref[at >> 3] * BLK + (at & 7) * 16
                out_ref[pl.ds(pl.multiple_of(row, 16), 16), :] = in_refs[r][
                    s, group * 16 : (group + 1) * 16, :
                ]


def order_rows(ffn_order, pieces):
    count, rows, width = pieces[0].shape
    return pl.pallas_call(
        order_kernel,
        out_shape=jax.ShapeDtypeStruct((4 * count * rows, width), jnp.bfloat16),
        in_specs=[pl.BlockSpec(memory_space=pltpu.SMEM)] + whole(4),
        out_specs=whole(1)[0],
        scratch_shapes=[pltpu.SMEM((FFB,), jnp.int32)],
        compiler_params=params(),
        cost_estimate=cost(4 * count * rows * width, 16 * count * rows * width),
        name="order_rows",
    )(ffn_order, *pieces)


def exchange(pieces, axes):
    return lax.all_to_all(pieces, axes, split_axis=0, concat_axis=0, tiled=True)


def exchange_z(pieces):
    got = list(pieces)
    for s in (4, 1, 7, 2, 6, 3, 5):
        got[s] = lax.ppermute(pieces[s], "z", [(i, (i + s) % DEEP) for i in range(DEEP)])
    return got


def exchange_side(pieces):
    got = list(pieces)
    for r in (1, 2, 3):
        got[r] = lax.ppermute(pieces[r], ("xh", "core"), [(i, i ^ r) for i in range(4)])
    return got


def exchange_core(got):
    return lax.ppermute(got, "core", [(0, 1), (1, 0)])


def tie(*arrays):
    return lax.optimization_barrier(arrays)


def per_device(
    q_weight,
    k_weight,
    v_weight,
    gate_weight,
    up_weight,
    down_weight,
    attn_gain,
    ffn_gain,
    head_order,
    ffn_order,
):
    shards = math.prod(lax.axis_size(name) for name in FSDP)
    columns = pick(
        head_order,
        ffn_order,
        [attn_gain, ffn_gain],
        [q_weight, k_weight, v_weight, gate_weight, up_weight],
    )
    columns = exchange(columns, PLANE)
    shifted = exchange_z(rotate_down(down_weight, shards))
    first = first_mix(columns, 0, UP_START)
    first, *packed = tie(first, *repack(shifted))
    first = exchange(first, DEPTH)
    second = first_mix(columns, UP_START, WIDTH - UP_START)
    moved = exchange_side(packed)
    second, first, *moved = tie(second, first, *moved)
    second = exchange(second, DEPTH)
    merged_ffn, merged_attn = last_mix(first, exchange_core(first), 0, True)
    merged_down = order_rows(ffn_order, moved)
    second, merged_ffn, merged_attn, merged_down = tie(second, merged_ffn, merged_attn, merged_down)
    (merged_ffn,) = last_mix(second, exchange_core(second), 2, False, merged_ffn)
    return (merged_attn, merged_ffn, merged_down)


def solution(mesh):
    split = Mesh(mesh.devices.reshape(2, 8, 2, 2, 4), ("xh", "z", "core", "xl", "y"))
    rows = TP + FSDP
    placed = (P(rows, None),) * 6 + (P(rows),) * 2 + (P(), P())
    return jax.shard_map(
        per_device,
        mesh=split,
        in_specs=placed,
        out_specs=(P(FSDP, TP), P(FSDP, TP), P(TP, FSDP)),
        check_vma=False,
    )
```

```python
import functools
import math

import jax
import jax.numpy as jnp
import numpy as np
from jax import lax
from jax.experimental import pallas as pl
from jax.experimental.pallas import tpu as pltpu
from jax.sharding import Mesh
from jax.sharding import PartitionSpec as P

BLK = 128
QPG = 8
FFB = 28
HALF_Q = QPG // 2
HALF_F = FFB // 2
ROWS = 32
PIECES = 16
DEEP = 8
SHIFTS = (0, 1, 7, 3, 5, 2, 6, 4)
FFN_WIDTH = HALF_F * BLK
HEADS_WIDTH = (HALF_Q + 1) * BLK
VMEM_LIMIT = 16 * 1024 * 1024
VMEM_MOST = 56 * 1024 * 1024
PLANE = ("xh", "xl", "y")
DEPTH = ("xh", "z")
FSDP = ("xh", "z", "core")
TP = ("xl", "y")


def signs(order):
    index = np.arange(order)
    common = index[:, None] & index[None, :]
    parity = np.zeros((order, order), np.int64)
    while common.any():
        parity ^= common & 1
        common = common >> 1
    return (1 - 2 * parity).astype(np.float32)


def bf16(values):
    return values.astype(jnp.bfloat16)


def params(limit=VMEM_LIMIT):
    return pltpu.CompilerParams(vmem_limit_bytes=limit)


def cost(flops, moved):
    return pl.CostEstimate(flops=int(flops), bytes_accessed=int(moved), transcendentals=0)


def side_index():
    return lax.axis_index("xh") * 2 + lax.axis_index("core")


def whole(count):
    return [pl.BlockSpec(memory_space=pltpu.VMEM)] * count


def pair_sums(values, span):
    out = list(values)
    for i in range(len(values)):
        if not i & span:
            out[i] = values[i] + values[i | span]
            out[i | span] = values[i] - values[i | span]
    return out


def down_kernel(weight_ref, sign_ref, *refs):
    out_refs, held_ref = refs[:DEEP], refs[DEEP]
    sign = sign_ref[...]
    groups = weight_ref.shape[1] // BLK
    side, z = side_index(), lax.axis_index("z")

    @pl.loop(0, weight_ref.shape[0] // 16)
    def _(step):
        rows = pl.ds(pl.multiple_of(step * 16, 16), 16)
        tall = jnp.concatenate(
            [weight_ref[rows, a * BLK : (a + 1) * BLK] for a in range(groups)], axis=0
        )
        half = jnp.dot(tall, sign, preferred_element_type=jnp.float32)
        half = bf16(half * (1.0 / math.sqrt(BLK))).astype(jnp.float32)
        parts = [half[a * 16 : (a + 1) * 16] for a in range(groups)]
        span = 1
        while span < groups:
            parts = pair_sums(parts, span)
            span *= 2
        for a in range(groups):
            held_ref[a] = bf16(parts[a] * (1.0 / math.sqrt(groups)))
        for at, s in enumerate(SHIFTS):
            for r in range(4):
                there = side ^ r
                shard = (there >> 1) * 2 * DEEP + ((z + s) & (DEEP - 1)) * 2 + (there & 1)
                for a in range(2):
                    out_refs[at][r, rows, a * BLK : (a + 1) * BLK] = held_ref[shard * 2 + a]


def rotate_down(weight, shards):
    rows, width = weight.shape
    groups = width // BLK
    return pl.pallas_call(
        down_kernel,
        out_shape=[jax.ShapeDtypeStruct((4, rows, width // shards), jnp.bfloat16)] * DEEP,
        in_specs=whole(2),
        out_specs=whole(DEEP),
        scratch_shapes=[pltpu.VMEM((groups, 16, BLK), jnp.bfloat16)],
        compiler_params=params(),
        cost_estimate=cost(2 * rows * width * BLK * 4, 4 * rows * width),
        name="down_rotate",
    )(weight, jnp.asarray(signs(BLK), jnp.bfloat16))


def repack_kernel(*refs):
    in_refs, out_refs = refs[:DEEP], refs[DEEP:]
    for r in range(4):
        for s in range(DEEP):
            out_refs[r][s] = in_refs[s][r]


def repack(pieces):
    _, rows, width = pieces[0].shape
    return pl.pallas_call(
        repack_kernel,
        out_shape=[jax.ShapeDtypeStruct((DEEP, rows, width), jnp.bfloat16)] * 4,
        in_specs=whole(DEEP),
        out_specs=whole(4),
        compiler_params=params(),
        cost_estimate=cost(4 * DEEP * rows * width, 16 * DEEP * rows * width),
        name="repack_down",
    )(*pieces)


def spread(gain_ref):
    row = lax.broadcasted_iota(jnp.int32, (ROWS, BLK), 0)
    spread_gain = jnp.zeros((ROWS, BLK), jnp.float32)
    for i in range(ROWS):
        spread_gain = jnp.where(row == i, gain_ref[i], spread_gain)
    return spread_gain


def scaled(ref, block, gain):
    columns = pl.ds(pl.multiple_of(block * BLK, BLK), BLK)
    return bf16(ref[:, columns].astype(jnp.float32) * gain)


def pick_kernel(with_heads, order_ref, ffn_gain_ref, ffn_ref, *refs):
    out_ref = refs[-1]
    ffn_gain = spread(ffn_gain_ref)
    if with_heads:
        heads_ref, attn_gain_ref, q_ref, k_ref, v_ref = refs[:-1]
        attn_gain = spread(attn_gain_ref)
    each = out_ref.shape[0]
    for j in range(each):
        piece = pl.program_id(0) * each + j
        owner, half = piece & 7, piece >> 3
        for slot in range(HALF_F):
            block = owner * FFB + order_ref[owner, half * HALF_F + slot]
            out_ref[j, :, slot * BLK : (slot + 1) * BLK] = scaled(ffn_ref, block, ffn_gain)
        if with_heads:
            for slot in range(HALF_Q):
                head = owner * QPG + heads_ref[owner, half * HALF_Q + slot]
                columns = slice(FFN_WIDTH + slot * BLK, FFN_WIDTH + (slot + 1) * BLK)
                out_ref[j, :, columns] = scaled(q_ref, head, attn_gain)
            out_ref[j, :, FFN_WIDTH + HALF_Q * BLK :] = jnp.where(
                half == 1, scaled(v_ref, owner, attn_gain), scaled(k_ref, owner, attn_gain)
            )


def pick(order, gain, weight, heads=()):
    each = 4
    width = FFN_WIDTH + (HEADS_WIDTH if heads else 0)
    small = pl.BlockSpec(memory_space=pltpu.SMEM)
    in_specs = [
        small if array.size < 1024 else pl.BlockSpec(array.shape, lambda i: (0, 0))
        for array in (order, gain, weight, *heads)
    ]
    return pl.pallas_call(
        functools.partial(pick_kernel, bool(heads)),
        grid=(PIECES // each,),
        out_shape=jax.ShapeDtypeStruct((PIECES, ROWS, width), jnp.bfloat16),
        in_specs=in_specs,
        out_specs=pl.BlockSpec((each, ROWS, width), lambda i: (i, 0, 0)),
        compiler_params=params(VMEM_MOST),
        cost_estimate=cost(PIECES * ROWS * width * 400, 4 * PIECES * ROWS * width),
        name="pick_columns",
    )(order, gain, weight, *heads)


def column_groups(widths, count):
    groups, begin = [], 0
    for at, width in enumerate(widths):
        step = -(-width // (count * BLK)) * BLK
        for start in range(0, width, step):
            groups.append((at, start, min(step, width - start), begin + start))
        begin += width
    return groups


def first_kernel(groups, matrix_ref, gates_ref, rest_ref, out_ref, in_held, out_held, in_sems, out_sems):
    in_copies, out_copies = [], []
    for at, (array, start, width, begin) in enumerate(groups):
        source = (gates_ref, rest_ref)[array].at[:, :, pl.ds(start, width)]
        there = pl.ds(begin, width)
        in_copies.append(
            pltpu.make_async_copy(source, in_held.at[:, :, there], in_sems.at[at])
        )
        out_copies.append(
            pltpu.make_async_copy(
                out_held.at[:, :, there], out_ref.at[:, :, there], out_sems.at[at]
            )
        )
    for copy in in_copies:
        copy.start()
    matrix = matrix_ref[...]
    for at, (_, _, width, begin) in enumerate(groups):
        in_copies[at].wait()
        for start in range(begin, begin + width, 2 * BLK):
            stop = min(start + 2 * BLK, begin + width)
            sides = [
                jnp.dot(
                    matrix,
                    in_held[side * 8 : side * 8 + 8, :, start:stop].reshape(8 * ROWS, -1),
                    preferred_element_type=jnp.float32,
                )
                for side in range(2)
            ]
            for which, mixed in enumerate((sides[0] + sides[1], sides[0] - sides[1])):
                mixed = bf16(mixed).reshape(8, ROWS, -1)
                for group in range(8):
                    out_held[2 * group + which, :, start:stop] = mixed[group]
        out_copies[at].start()
    for copy in out_copies:
        copy.wait()


def first_mix(gates, rest):
    rows = 8 * ROWS
    widths = (gates.shape[2], rest.shape[2])
    width = sum(widths)
    groups = column_groups(widths, 2)
    held = pltpu.VMEM((PIECES, ROWS, width), jnp.bfloat16)
    sems = pltpu.SemaphoreType.DMA((len(groups),))
    return pl.pallas_call(
        functools.partial(first_kernel, groups),
        out_shape=jax.ShapeDtypeStruct((PIECES, ROWS, width), jnp.bfloat16),
        in_specs=whole(1) + [pl.BlockSpec(memory_space=pl.ANY)] * 2,
        out_specs=pl.BlockSpec(memory_space=pl.ANY),
        scratch_shapes=[held, held, sems, sems],
        compiler_params=params(VMEM_MOST),
        cost_estimate=cost(4 * rows * rows * width, 8 * rows * width),
        name="first_mix",
    )(jnp.asarray(signs(rows) / 16.0, jnp.bfloat16), gates, rest)


def core_sign():
    return (1 - 2 * lax.axis_index("core")).astype(jnp.float32)


def side_sums(sign, ref, part, columns):
    rows = [ref[part * 8 + j, :, columns].astype(jnp.float32) for j in range(8)]
    rows = [rows[j] + sign * rows[j + 4] for j in range(4)]
    return pair_sums(pair_sums(rows, 2), 1)


def own_kernel(own_ref, out_ref, held, sems):
    sign = core_sign()
    copies = [
        pltpu.make_async_copy(
            own_ref.at[pl.ds(part * 8, 8)], held.at[pl.ds(part * 8, 8)], sems.at[part]
        )
        for part in range(2)
    ]
    for copy in copies:
        copy.start()
    for part in range(2):
        copies[part].wait()

        @pl.loop(0, held.shape[2] // BLK)
        def _(step):
            columns = pl.ds(pl.multiple_of(step * BLK, BLK), BLK)
            for j, value in enumerate(side_sums(sign, held, part, columns)):
                out_ref[part * 4 + j, :, columns] = value


def own_sums(own):
    width = own.shape[2]
    return pl.pallas_call(
        own_kernel,
        out_shape=jax.ShapeDtypeStruct((8, ROWS, width), jnp.float32),
        in_specs=[pl.BlockSpec(memory_space=pl.ANY)],
        out_specs=whole(1)[0],
        scratch_shapes=[pltpu.VMEM(own.shape, jnp.bfloat16), pltpu.SemaphoreType.DMA((2,))],
        compiler_params=params(),
        cost_estimate=cost(40 * own.size, 4 * own.size),
        name="own_sums",
    )(own)


def last_columns(sign, sums_ref, other_ref, part, columns):
    theirs = side_sums(sign, other_ref, part, columns)
    scale = 16.0 / math.sqrt(8192.0)
    parts = []
    for j in range(4):
        mine = sums_ref[part * 4 + j, :, columns]
        parts.append(bf16((mine + theirs[j]) * scale))
        parts.append(bf16((mine - theirs[j]) * (scale * sign)))
    return jnp.concatenate(parts, axis=0)


def last_kernel(sums_ref, other_ref, ffn_ref, heads_ref):
    sign = core_sign()
    part = pl.program_id(0) & 1
    begin = (pl.program_id(0) >> 1) * HALF_F

    @pl.loop(0, HALF_F // 2)
    def _(step):
        columns = pl.ds(pl.multiple_of(step * 2 * BLK, 2 * BLK), 2 * BLK)
        source = pl.ds(pl.multiple_of((begin + step * 2) * BLK, 2 * BLK), 2 * BLK)
        ffn_ref[:, columns] = last_columns(sign, sums_ref, other_ref, part, source)

    @pl.when(pl.program_id(0) == 0)
    def _():
        for half in range(2):
            for slot in range(HALF_Q + 1):
                block = half * HALF_Q + slot if slot < HALF_Q else QPG + half
                source = slice(2 * FFN_WIDTH + slot * BLK, 2 * FFN_WIDTH + (slot + 1) * BLK)
                heads_ref[:, block * BLK : (block + 1) * BLK] = last_columns(
                    sign, sums_ref, other_ref, half, source
                )


def last_mix(sums, other):
    rows = 8 * ROWS
    width = 4 * FFN_WIDTH
    return pl.pallas_call(
        last_kernel,
        grid=(4,),
        out_shape=[
            jax.ShapeDtypeStruct((rows, width), jnp.bfloat16),
            jax.ShapeDtypeStruct((rows, 2 * HEADS_WIDTH), jnp.bfloat16),
        ],
        in_specs=whole(2),
        out_specs=[
            pl.BlockSpec((rows, FFN_WIDTH), lambda i: (0, i)),
            pl.BlockSpec((rows, 2 * HEADS_WIDTH), lambda i: (0, 0)),
        ],
        compiler_params=params(),
        cost_estimate=cost(40 * rows * width, 6 * rows * width),
        name="last_mix",
    )(sums, other)


def order_kernel(order_ref, *refs):
    in_refs, (out_ref, slot_ref) = refs[:4], refs[4:]
    owner = lax.axis_index("xl") * 4 + lax.axis_index("y")
    side, z = side_index(), lax.axis_index("z")
    for slot in range(FFB):
        slot_ref[order_ref[owner, slot]] = slot
    groups = in_refs[0].shape[1] // 16
    for r in range(4):
        there = side ^ r
        for place, s in enumerate(SHIFTS):
            shard = (there >> 1) * 2 * DEEP + ((z - s) & (DEEP - 1)) * 2 + (there & 1)
            for group in range(groups):
                at = shard * groups + group
                row = slot_ref[at >> 3] * BLK + (at & 7) * 16
                out_ref[pl.ds(pl.multiple_of(row, 16), 16), :] = in_refs[r][
                    place, group * 16 : (group + 1) * 16, :
                ]


def order_rows(ffn_order, pieces):
    count, rows, width = pieces[0].shape
    return pl.pallas_call(
        order_kernel,
        out_shape=jax.ShapeDtypeStruct((4 * count * rows, width), jnp.bfloat16),
        in_specs=[pl.BlockSpec(memory_space=pltpu.SMEM)] + whole(4),
        out_specs=whole(1)[0],
        scratch_shapes=[pltpu.SMEM((FFB,), jnp.int32)],
        compiler_params=params(),
        cost_estimate=cost(4 * count * rows * width, 16 * count * rows * width),
        name="order_rows",
    )(ffn_order, *pieces)


def exchange(pieces, axes):
    return lax.all_to_all(pieces, axes, split_axis=0, concat_axis=0, tiled=True)


def exchange_apart(go, pieces, axes):
    return lax.cond(go, lambda part: exchange(part, axes), jnp.zeros_like, pieces)


def exchange_z(pieces):
    got = list(pieces)
    for at, s in enumerate(SHIFTS):
        if s:
            got[at] = lax.ppermute(pieces[at], "z", [(i, (i + s) % DEEP) for i in range(DEEP)])
    return got


def exchange_side(pieces):
    got = list(pieces)
    for r in (1, 2, 3):
        got[r] = lax.ppermute(pieces[r], ("xh", "core"), [(i, i ^ r) for i in range(4)])
    return got


def exchange_core(got):
    return lax.ppermute(got, "core", [(0, 1), (1, 0)])


def tie(*arrays):
    return lax.optimization_barrier(arrays)


def per_device(
    q_weight,
    k_weight,
    v_weight,
    gate_weight,
    up_weight,
    down_weight,
    attn_gain,
    ffn_gain,
    head_order,
    ffn_order,
):
    shards = math.prod(lax.axis_size(name) for name in FSDP)
    go = lax.axis_index("z") >= 0
    gates = exchange(pick(ffn_order, ffn_gain, gate_weight), PLANE)
    heads = (head_order, attn_gain, q_weight, k_weight, v_weight)
    rest = pick(ffn_order, ffn_gain, up_weight, heads)
    shifted = exchange_z(rotate_down(down_weight, shards))
    rest, gates = tie(rest, gates)
    rest, *shifted = tie(exchange_apart(go, rest, PLANE), *shifted)
    mixed, *packed = tie(first_mix(gates, rest), *repack(shifted))
    mixed = exchange_apart(go, mixed, DEPTH)
    moved = exchange_side(packed)
    mixed, *moved = tie(mixed, *moved)
    other = exchange_core(mixed)
    merged_down = order_rows(ffn_order, moved)
    merged_ffn, merged_attn = last_mix(own_sums(mixed), other)
    return (merged_attn, merged_ffn, merged_down)


def solution(mesh):
    split = Mesh(mesh.devices.reshape(2, 8, 2, 2, 4), ("xh", "z", "core", "xl", "y"))
    rows = TP + FSDP
    placed = (P(rows, None),) * 6 + (P(rows),) * 2 + (P(), P())
    return jax.shard_map(
        per_device,
        mesh=split,
        in_specs=placed,
        out_specs=(P(FSDP, TP), P(FSDP, TP), P(TP, FSDP)),
        check_vma=False,
    )
```

```python
import functools
import math

import jax
import jax.numpy as jnp
import numpy as np
from jax import lax
from jax.experimental import pallas as pl
from jax.experimental.pallas import tpu as pltpu
from jax.sharding import Mesh
from jax.sharding import PartitionSpec as P

BLK = 128
QPG = 8
FFB = 28
HALF_Q = QPG // 2
HALF_F = FFB // 2
ROWS = 32
PIECES = 16
DEEP = 8
SHIFTS = (0, 1, 7, 3, 5, 2, 6, 4)
FFN_WIDTH = HALF_F * BLK
HEADS_WIDTH = (HALF_Q + 1) * BLK
VMEM_LIMIT = 16 * 1024 * 1024
VMEM_MOST = 56 * 1024 * 1024
PLANE = ("xh", "xl", "y")
DEPTH = ("xh", "z")
FSDP = ("xh", "z", "core")
TP = ("xl", "y")


def signs(order):
    index = np.arange(order)
    common = index[:, None] & index[None, :]
    parity = np.zeros((order, order), np.int64)
    while common.any():
        parity ^= common & 1
        common = common >> 1
    return (1 - 2 * parity).astype(np.float32)


def bf16(values):
    return values.astype(jnp.bfloat16)


def params(limit=VMEM_LIMIT):
    return pltpu.CompilerParams(vmem_limit_bytes=limit)


def cost(flops, moved):
    return pl.CostEstimate(flops=int(flops), bytes_accessed=int(moved), transcendentals=0)


def side_index():
    return lax.axis_index("xh") * 2 + lax.axis_index("core")


def whole(count):
    return [pl.BlockSpec(memory_space=pltpu.VMEM)] * count


def pair_sums(values, span):
    out = list(values)
    for i in range(len(values)):
        if not i & span:
            out[i] = values[i] + values[i | span]
            out[i | span] = values[i] - values[i | span]
    return out


def down_kernel(weight_ref, sign_ref, *refs):
    out_refs, held_ref = refs[:DEEP], refs[DEEP]
    sign = sign_ref[...]
    groups = weight_ref.shape[1] // BLK
    side, z = side_index(), lax.axis_index("z")

    @pl.loop(0, weight_ref.shape[0] // 16)
    def _(step):
        rows = pl.ds(pl.multiple_of(step * 16, 16), 16)
        tall = jnp.concatenate(
            [weight_ref[rows, a * BLK : (a + 1) * BLK] for a in range(groups)], axis=0
        )
        half = jnp.dot(tall, sign, preferred_element_type=jnp.float32)
        half = bf16(half * (1.0 / math.sqrt(BLK))).astype(jnp.float32)
        parts = [half[a * 16 : (a + 1) * 16] for a in range(groups)]
        span = 1
        while span < groups:
            parts = pair_sums(parts, span)
            span *= 2
        for a in range(groups):
            held_ref[a] = bf16(parts[a] * (1.0 / math.sqrt(groups)))
        for at, s in enumerate(SHIFTS):
            for r in range(4):
                there = side ^ r
                shard = (there >> 1) * 2 * DEEP + ((z + s) & (DEEP - 1)) * 2 + (there & 1)
                for a in range(2):
                    out_refs[at][r, rows, a * BLK : (a + 1) * BLK] = held_ref[shard * 2 + a]


def rotate_down(weight, shards):
    rows, width = weight.shape
    groups = width // BLK
    return pl.pallas_call(
        down_kernel,
        out_shape=[jax.ShapeDtypeStruct((4, rows, width // shards), jnp.bfloat16)] * DEEP,
        in_specs=whole(2),
        out_specs=whole(DEEP),
        scratch_shapes=[pltpu.VMEM((groups, 16, BLK), jnp.bfloat16)],
        compiler_params=params(),
        cost_estimate=cost(2 * rows * width * BLK * 4, 4 * rows * width),
        name="down_rotate",
    )(weight, jnp.asarray(signs(BLK), jnp.bfloat16))


def repack_kernel(*refs):
    in_refs, out_refs = refs[:DEEP], refs[DEEP:]
    for r in range(4):
        for s in range(DEEP):
            out_refs[r][s] = in_refs[s][r]


def repack(pieces):
    _, rows, width = pieces[0].shape
    return pl.pallas_call(
        repack_kernel,
        out_shape=[jax.ShapeDtypeStruct((DEEP, rows, width), jnp.bfloat16)] * 4,
        in_specs=whole(DEEP),
        out_specs=whole(4),
        compiler_params=params(),
        cost_estimate=cost(4 * DEEP * rows * width, 16 * DEEP * rows * width),
        name="repack_down",
    )(*pieces)


def spread(gain_ref):
    row = lax.broadcasted_iota(jnp.int32, (ROWS, BLK), 0)
    spread_gain = jnp.zeros((ROWS, BLK), jnp.float32)
    for i in range(ROWS):
        spread_gain = jnp.where(row == i, gain_ref[i], spread_gain)
    return spread_gain


def scaled(ref, block, gain):
    columns = pl.ds(pl.multiple_of(block * BLK, BLK), BLK)
    return bf16(ref[:, columns].astype(jnp.float32) * gain)


def pick_kernel(with_heads, order_ref, ffn_gain_ref, ffn_ref, *refs):
    out_ref = refs[-1]
    ffn_gain = spread(ffn_gain_ref)
    if with_heads:
        heads_ref, attn_gain_ref, q_ref, k_ref, v_ref = refs[:-1]
        attn_gain = spread(attn_gain_ref)
    each = out_ref.shape[0]
    for j in range(each):
        owner, half = j, pl.program_id(0)
        for slot in range(HALF_F):
            block = owner * FFB + order_ref[owner, half * HALF_F + slot]
            out_ref[j, :, slot * BLK : (slot + 1) * BLK] = scaled(ffn_ref, block, ffn_gain)
        if with_heads:
            for slot in range(HALF_Q):
                head = owner * QPG + heads_ref[owner, half * HALF_Q + slot]
                columns = slice(FFN_WIDTH + slot * BLK, FFN_WIDTH + (slot + 1) * BLK)
                out_ref[j, :, columns] = scaled(q_ref, head, attn_gain)
            out_ref[j, :, FFN_WIDTH + HALF_Q * BLK :] = jnp.where(
                half == 1, scaled(v_ref, owner, attn_gain), scaled(k_ref, owner, attn_gain)
            )


def pick(order, gain, weight, heads=()):
    each = 8
    width = FFN_WIDTH + (HEADS_WIDTH if heads else 0)
    small = pl.BlockSpec(memory_space=pltpu.SMEM)
    in_specs = [
        small if array.size < 1024 else pl.BlockSpec(array.shape, lambda i: (0, 0))
        for array in (order, gain, weight, *heads)
    ]
    return pl.pallas_call(
        functools.partial(pick_kernel, bool(heads)),
        grid=(PIECES // each,),
        out_shape=jax.ShapeDtypeStruct((PIECES, ROWS, width), jnp.bfloat16),
        in_specs=in_specs,
        out_specs=pl.BlockSpec((each, ROWS, width), lambda i: (i, 0, 0)),
        compiler_params=params(VMEM_MOST),
        cost_estimate=cost(PIECES * ROWS * width * 400, 4 * PIECES * ROWS * width),
        name="pick_columns",
    )(order, gain, weight, *heads)


def column_groups(widths, count):
    groups, begin = [], 0
    for at, width in enumerate(widths):
        step = -(-width // (count * BLK)) * BLK
        for start in range(0, width, step):
            groups.append((at, start, min(step, width - start), begin + start))
        begin += width
    return groups


def first_kernel(groups, matrix_ref, gates_ref, rest_ref, out_ref, in_held, out_held, in_sems, out_sems):
    in_copies, out_copies = [], []
    for at, (array, start, width, begin) in enumerate(groups):
        source = (gates_ref, rest_ref)[array].at[:, :, pl.ds(start, width)]
        there = pl.ds(begin, width)
        in_copies.append(
            pltpu.make_async_copy(source, in_held.at[:, :, there], in_sems.at[at])
        )
        out_copies.append(
            pltpu.make_async_copy(
                out_held.at[:, :, there], out_ref.at[:, :, there], out_sems.at[at]
            )
        )
    for copy in in_copies:
        copy.start()
    matrix = matrix_ref[...]
    for at, (_, _, width, begin) in enumerate(groups):
        in_copies[at].wait()
        for start in range(begin, begin + width, 2 * BLK):
            stop = min(start + 2 * BLK, begin + width)
            sides = [
                jnp.dot(
                    matrix,
                    in_held[side * 8 : side * 8 + 8, :, start:stop].reshape(8 * ROWS, -1),
                    preferred_element_type=jnp.float32,
                )
                for side in range(2)
            ]
            for which, mixed in enumerate((sides[0] + sides[1], sides[0] - sides[1])):
                mixed = bf16(mixed).reshape(8, ROWS, -1)
                for group in range(8):
                    out_held[2 * group + which, :, start:stop] = mixed[group]
        out_copies[at].start()
    for copy in out_copies:
        copy.wait()


def first_mix(gates, rest):
    rows = 8 * ROWS
    widths = (gates.shape[2], rest.shape[2])
    width = sum(widths)
    groups = column_groups(widths, 2)
    held = pltpu.VMEM((PIECES, ROWS, width), jnp.bfloat16)
    sems = pltpu.SemaphoreType.DMA((len(groups),))
    return pl.pallas_call(
        functools.partial(first_kernel, groups),
        out_shape=jax.ShapeDtypeStruct((PIECES, ROWS, width), jnp.bfloat16),
        in_specs=whole(1) + [pl.BlockSpec(memory_space=pl.ANY)] * 2,
        out_specs=pl.BlockSpec(memory_space=pl.ANY),
        scratch_shapes=[held, held, sems, sems],
        compiler_params=params(VMEM_MOST),
        cost_estimate=cost(4 * rows * rows * width, 8 * rows * width),
        name="first_mix",
    )(jnp.asarray(signs(rows) / 16.0, jnp.bfloat16), gates, rest)


def core_sign():
    return (1 - 2 * lax.axis_index("core")).astype(jnp.float32)


def side_sums(sign, ref, part, columns):
    rows = [ref[part * 8 + j, :, columns].astype(jnp.float32) for j in range(8)]
    rows = [rows[j] + sign * rows[j + 4] for j in range(4)]
    return pair_sums(pair_sums(rows, 2), 1)


def own_kernel(own_ref, out_ref, held, sems):
    sign = core_sign()
    copies = [
        pltpu.make_async_copy(
            own_ref.at[pl.ds(part * 8, 8)], held.at[pl.ds(part * 8, 8)], sems.at[part]
        )
        for part in range(2)
    ]
    for copy in copies:
        copy.start()
    for part in range(2):
        copies[part].wait()

        @pl.loop(0, held.shape[2] // BLK)
        def _(step):
            columns = pl.ds(pl.multiple_of(step * BLK, BLK), BLK)
            for j, value in enumerate(side_sums(sign, held, part, columns)):
                out_ref[part * 4 + j, :, columns] = value


def own_sums(own):
    width = own.shape[2]
    return pl.pallas_call(
        own_kernel,
        out_shape=jax.ShapeDtypeStruct((8, ROWS, width), jnp.float32),
        in_specs=[pl.BlockSpec(memory_space=pl.ANY)],
        out_specs=whole(1)[0],
        scratch_shapes=[pltpu.VMEM(own.shape, jnp.bfloat16), pltpu.SemaphoreType.DMA((2,))],
        compiler_params=params(),
        cost_estimate=cost(40 * own.size, 4 * own.size),
        name="own_sums",
    )(own)


def last_columns(sign, sums_ref, other_ref, part, columns):
    theirs = side_sums(sign, other_ref, part, columns)
    scale = 16.0 / math.sqrt(8192.0)
    parts = []
    for j in range(4):
        mine = sums_ref[part * 4 + j, :, columns]
        parts.append(bf16((mine + theirs[j]) * scale))
        parts.append(bf16((mine - theirs[j]) * (scale * sign)))
    return jnp.concatenate(parts, axis=0)


def last_kernel(sums_ref, other_ref, ffn_ref, heads_ref):
    sign = core_sign()
    part = pl.program_id(0) & 1
    begin = (pl.program_id(0) >> 1) * HALF_F

    for step in range(0, HALF_F, 2):
        source = pl.ds(pl.multiple_of((begin + step) * BLK, 2 * BLK), 2 * BLK)
        ffn_ref[:, step * BLK : (step + 2) * BLK] = last_columns(
            sign, sums_ref, other_ref, part, source
        )

    @pl.when(pl.program_id(0) == 0)
    def _():
        for half in range(2):
            for slot in range(HALF_Q + 1):
                block = half * HALF_Q + slot if slot < HALF_Q else QPG + half
                source = slice(2 * FFN_WIDTH + slot * BLK, 2 * FFN_WIDTH + (slot + 1) * BLK)
                heads_ref[:, block * BLK : (block + 1) * BLK] = last_columns(
                    sign, sums_ref, other_ref, half, source
                )


def last_mix(sums, other):
    rows = 8 * ROWS
    width = 4 * FFN_WIDTH
    return pl.pallas_call(
        last_kernel,
        grid=(4,),
        out_shape=[
            jax.ShapeDtypeStruct((rows, width), jnp.bfloat16),
            jax.ShapeDtypeStruct((rows, 2 * HEADS_WIDTH), jnp.bfloat16),
        ],
        in_specs=whole(2),
        out_specs=[
            pl.BlockSpec((rows, FFN_WIDTH), lambda i: (0, i)),
            pl.BlockSpec((rows, 2 * HEADS_WIDTH), lambda i: (0, 0)),
        ],
        compiler_params=params(),
        cost_estimate=cost(40 * rows * width, 6 * rows * width),
        name="last_mix",
    )(sums, other)


def order_kernel(order_ref, *refs):
    in_refs, (out_ref, slot_ref) = refs[:4], refs[4:]
    owner = lax.axis_index("xl") * 4 + lax.axis_index("y")
    side, z = side_index(), lax.axis_index("z")
    for slot in range(FFB):
        slot_ref[order_ref[owner, slot]] = slot
    groups = in_refs[0].shape[1] // 16
    for r in range(4):
        there = side ^ r
        for place, s in enumerate(SHIFTS):
            shard = (there >> 1) * 2 * DEEP + ((z - s) & (DEEP - 1)) * 2 + (there & 1)
            for group in range(groups):
                at = shard * groups + group
                row = slot_ref[at >> 3] * BLK + (at & 7) * 16
                out_ref[pl.ds(pl.multiple_of(row, 16), 16), :] = in_refs[r][
                    place, group * 16 : (group + 1) * 16, :
                ]


def order_rows(ffn_order, pieces):
    count, rows, width = pieces[0].shape
    return pl.pallas_call(
        order_kernel,
        out_shape=jax.ShapeDtypeStruct((4 * count * rows, width), jnp.bfloat16),
        in_specs=[pl.BlockSpec(memory_space=pltpu.SMEM)] + whole(4),
        out_specs=whole(1)[0],
        scratch_shapes=[pltpu.SMEM((FFB,), jnp.int32)],
        compiler_params=params(),
        cost_estimate=cost(4 * count * rows * width, 16 * count * rows * width),
        name="order_rows",
    )(ffn_order, *pieces)


def exchange(pieces, axes):
    return lax.all_to_all(pieces, axes, split_axis=0, concat_axis=0, tiled=True)


def exchange_apart(go, pieces, axes):
    return lax.cond(go, lambda part: exchange(part, axes), jnp.zeros_like, pieces)


def exchange_z(pieces):
    got = list(pieces)
    for at, s in enumerate(SHIFTS):
        if s:
            got[at] = lax.ppermute(pieces[at], "z", [(i, (i + s) % DEEP) for i in range(DEEP)])
    return got


def exchange_side(pieces, sides):
    got = list(pieces)
    for r in sides:
        got[r] = lax.ppermute(pieces[r], ("xh", "core"), [(i, i ^ r) for i in range(4)])
    return got


def exchange_core(got):
    return lax.ppermute(got, "core", [(0, 1), (1, 0)])


def tie(*arrays):
    return lax.optimization_barrier(arrays)


def per_device(
    q_weight,
    k_weight,
    v_weight,
    gate_weight,
    up_weight,
    down_weight,
    attn_gain,
    ffn_gain,
    head_order,
    ffn_order,
):
    shards = math.prod(lax.axis_size(name) for name in FSDP)
    go = lax.axis_index("z") >= 0
    gates = exchange(pick(ffn_order, ffn_gain, gate_weight), PLANE)
    heads = (head_order, attn_gain, q_weight, k_weight, v_weight)
    rest = pick(ffn_order, ffn_gain, up_weight, heads)
    shifted = exchange_z(rotate_down(down_weight, shards))
    rest, gates = tie(rest, gates)
    rest, *shifted = tie(exchange_apart(go, rest, PLANE), *shifted)
    mixed, *packed = tie(first_mix(gates, rest), *repack(shifted))
    mixed = exchange_apart(go, mixed, DEPTH)
    moved = exchange_side(packed, (2, 3))
    mixed, *moved = tie(mixed, *moved)
    other = exchange_core(mixed)
    moved = exchange_side(moved, (1,))
    merged_down = order_rows(ffn_order, moved)
    merged_ffn, merged_attn = last_mix(own_sums(mixed), other)
    return (merged_attn, merged_ffn, merged_down)


def solution(mesh):
    split = Mesh(mesh.devices.reshape(2, 8, 2, 2, 4), ("xh", "z", "core", "xl", "y"))
    rows = TP + FSDP
    placed = (P(rows, None),) * 6 + (P(rows),) * 2 + (P(), P())
    return jax.shard_map(
        per_device,
        mesh=split,
        in_specs=placed,
        out_specs=(P(FSDP, TP), P(FSDP, TP), P(TP, FSDP)),
        check_vma=False,
    )
```

```python
import functools
import math

import jax
import jax.numpy as jnp
import numpy as np
from jax import lax
from jax.experimental import pallas as pl
from jax.experimental.pallas import tpu as pltpu
from jax.sharding import Mesh
from jax.sharding import PartitionSpec as P

BLK = 128
QPG = 8
FFB = 28
HALF_Q = QPG // 2
HALF_F = FFB // 2
ROWS = 32
PIECES = 16
DEEP = 8
SHIFTS = (0, 1, 7, 3, 5, 2, 6, 4)
FFN_WIDTH = HALF_F * BLK
HEADS_WIDTH = (HALF_Q + 1) * BLK
VMEM_LIMIT = 16 * 1024 * 1024
VMEM_MOST = 56 * 1024 * 1024
PLANE = ("xh", "xl", "y")
DEPTH = ("xh", "z")
FSDP = ("xh", "z", "core")
TP = ("xl", "y")


def signs(order):
    index = np.arange(order)
    common = index[:, None] & index[None, :]
    parity = np.zeros((order, order), np.int64)
    while common.any():
        parity ^= common & 1
        common = common >> 1
    return (1 - 2 * parity).astype(np.float32)


def bf16(values):
    return values.astype(jnp.bfloat16)


def params(limit=VMEM_LIMIT):
    return pltpu.CompilerParams(vmem_limit_bytes=limit)


def cost(flops, moved):
    return pl.CostEstimate(flops=int(flops), bytes_accessed=int(moved), transcendentals=0)


def side_index():
    return lax.axis_index("xh") * 2 + lax.axis_index("core")


def whole(count):
    return [pl.BlockSpec(memory_space=pltpu.VMEM)] * count


def pair_sums(values, span):
    out = list(values)
    for i in range(len(values)):
        if not i & span:
            out[i] = values[i] + values[i | span]
            out[i | span] = values[i] - values[i | span]
    return out


def down_kernel(weight_ref, sign_ref, *refs):
    out_refs, held_ref = refs[:DEEP], refs[DEEP]
    sign = sign_ref[...]
    groups = weight_ref.shape[1] // BLK
    side, z = side_index(), lax.axis_index("z")

    @pl.loop(0, weight_ref.shape[0] // 16)
    def _(step):
        rows = pl.ds(pl.multiple_of(step * 16, 16), 16)
        tall = jnp.concatenate(
            [weight_ref[rows, a * BLK : (a + 1) * BLK] for a in range(groups)], axis=0
        )
        half = jnp.dot(tall, sign, preferred_element_type=jnp.float32)
        half = bf16(half * (1.0 / math.sqrt(BLK))).astype(jnp.float32)
        parts = [half[a * 16 : (a + 1) * 16] for a in range(groups)]
        span = 1
        while span < groups:
            parts = pair_sums(parts, span)
            span *= 2
        for a in range(groups):
            held_ref[a] = bf16(parts[a] * (1.0 / math.sqrt(groups)))
        for at, s in enumerate(SHIFTS):
            for r in range(4):
                there = side ^ r
                shard = (there >> 1) * 2 * DEEP + ((z + s) & (DEEP - 1)) * 2 + (there & 1)
                for a in range(2):
                    out_refs[at][r, rows, a * BLK : (a + 1) * BLK] = held_ref[shard * 2 + a]


def rotate_down(weight, shards):
    rows, width = weight.shape
    groups = width // BLK
    return pl.pallas_call(
        down_kernel,
        out_shape=[jax.ShapeDtypeStruct((4, rows, width // shards), jnp.bfloat16)] * DEEP,
        in_specs=whole(2),
        out_specs=whole(DEEP),
        scratch_shapes=[pltpu.VMEM((groups, 16, BLK), jnp.bfloat16)],
        compiler_params=params(),
        cost_estimate=cost(2 * rows * width * BLK * 4, 4 * rows * width),
        name="down_rotate",
    )(weight, jnp.asarray(signs(BLK), jnp.bfloat16))


def repack_kernel(*refs):
    in_refs, out_refs = refs[:DEEP], refs[DEEP:]
    for r in range(4):
        for s in range(DEEP):
            out_refs[r][s] = in_refs[s][r]


def repack(pieces):
    _, rows, width = pieces[0].shape
    return pl.pallas_call(
        repack_kernel,
        out_shape=[jax.ShapeDtypeStruct((DEEP, rows, width), jnp.bfloat16)] * 4,
        in_specs=whole(DEEP),
        out_specs=whole(4),
        compiler_params=params(),
        cost_estimate=cost(4 * DEEP * rows * width, 16 * DEEP * rows * width),
        name="repack_down",
    )(*pieces)


def spread(gain_ref):
    row = lax.broadcasted_iota(jnp.int32, (ROWS, BLK), 0)
    spread_gain = jnp.zeros((ROWS, BLK), jnp.float32)
    for i in range(ROWS):
        spread_gain = jnp.where(row == i, gain_ref[i], spread_gain)
    return spread_gain


def scaled(ref, block, gain):
    columns = pl.ds(pl.multiple_of(block * BLK, BLK), BLK)
    return bf16(ref[:, columns].astype(jnp.float32) * gain)


def pick_kernel(with_heads, order_ref, ffn_gain_ref, ffn_ref, *refs):
    out_ref = refs[-1]
    ffn_gain = spread(ffn_gain_ref)
    if with_heads:
        heads_ref, attn_gain_ref, q_ref, k_ref, v_ref = refs[:-1]
        attn_gain = spread(attn_gain_ref)
    each = out_ref.shape[0]
    for j in range(each):
        owner, half = j, pl.program_id(0)
        for slot in range(HALF_F):
            block = owner * FFB + order_ref[owner, half * HALF_F + slot]
            out_ref[j, :, slot * BLK : (slot + 1) * BLK] = scaled(ffn_ref, block, ffn_gain)
        if with_heads:
            for slot in range(HALF_Q):
                head = owner * QPG + heads_ref[owner, half * HALF_Q + slot]
                columns = slice(FFN_WIDTH + slot * BLK, FFN_WIDTH + (slot + 1) * BLK)
                out_ref[j, :, columns] = scaled(q_ref, head, attn_gain)
            out_ref[j, :, FFN_WIDTH + HALF_Q * BLK :] = jnp.where(
                half == 1, scaled(v_ref, owner, attn_gain), scaled(k_ref, owner, attn_gain)
            )


def pick(order, gain, weight, heads=()):
    each = 8
    width = FFN_WIDTH + (HEADS_WIDTH if heads else 0)
    small = pl.BlockSpec(memory_space=pltpu.SMEM)
    in_specs = [
        small if array.size < 1024 else pl.BlockSpec(array.shape, lambda i: (0, 0))
        for array in (order, gain, weight, *heads)
    ]
    return pl.pallas_call(
        functools.partial(pick_kernel, bool(heads)),
        grid=(PIECES // each,),
        out_shape=jax.ShapeDtypeStruct((PIECES, ROWS, width), jnp.bfloat16),
        in_specs=in_specs,
        out_specs=pl.BlockSpec((each, ROWS, width), lambda i: (i, 0, 0)),
        compiler_params=params(VMEM_MOST),
        cost_estimate=cost(PIECES * ROWS * width * 400, 4 * PIECES * ROWS * width),
        name="pick_columns",
    )(order, gain, weight, *heads)


def column_groups(widths, count):
    groups, begin = [], 0
    for at, width in enumerate(widths):
        step = -(-width // (count * BLK)) * BLK
        for start in range(0, width, step):
            groups.append((at, start, min(step, width - start), begin + start))
        begin += width
    return groups


def first_kernel(groups, matrix_ref, gates_ref, rest_ref, out_ref, in_held, out_held, in_sems, out_sems):
    in_copies, out_copies = [], []
    for at, (array, start, width, begin) in enumerate(groups):
        source = (gates_ref, rest_ref)[array].at[:, :, pl.ds(start, width)]
        there = pl.ds(begin, width)
        in_copies.append(
            pltpu.make_async_copy(source, in_held.at[:, :, there], in_sems.at[at])
        )
        out_copies.append(
            pltpu.make_async_copy(
                out_held.at[:, :, there], out_ref.at[:, :, there], out_sems.at[at]
            )
        )
    for copy in in_copies:
        copy.start()
    matrix = matrix_ref[...]
    for at, (_, _, width, begin) in enumerate(groups):
        in_copies[at].wait()
        for start in range(begin, begin + width, 2 * BLK):
            stop = min(start + 2 * BLK, begin + width)
            sides = [
                jnp.dot(
                    matrix,
                    in_held[side * 8 : side * 8 + 8, :, start:stop].reshape(8 * ROWS, -1),
                    preferred_element_type=jnp.float32,
                )
                for side in range(2)
            ]
            for which, mixed in enumerate((sides[0] + sides[1], sides[0] - sides[1])):
                mixed = bf16(mixed).reshape(8, ROWS, -1)
                for group in range(8):
                    out_held[2 * group + which, :, start:stop] = mixed[group]
        out_copies[at].start()
    for copy in out_copies:
        copy.wait()


def first_mix(gates, rest):
    rows = 8 * ROWS
    widths = (gates.shape[2], rest.shape[2])
    width = sum(widths)
    groups = column_groups(widths, 2)
    held = pltpu.VMEM((PIECES, ROWS, width), jnp.bfloat16)
    sems = pltpu.SemaphoreType.DMA((len(groups),))
    return pl.pallas_call(
        functools.partial(first_kernel, groups),
        out_shape=jax.ShapeDtypeStruct((PIECES, ROWS, width), jnp.bfloat16),
        in_specs=whole(1) + [pl.BlockSpec(memory_space=pl.ANY)] * 2,
        out_specs=pl.BlockSpec(memory_space=pl.ANY),
        scratch_shapes=[held, held, sems, sems],
        compiler_params=params(VMEM_MOST),
        cost_estimate=cost(4 * rows * rows * width, 8 * rows * width),
        name="first_mix",
    )(jnp.asarray(signs(rows) / 16.0, jnp.bfloat16), gates, rest)


def core_sign():
    return (1 - 2 * lax.axis_index("core")).astype(jnp.float32)


def own_kernel(part, own_ref, mine_ref, send_ref, held, sem):
    sign = core_sign()
    copy = pltpu.make_async_copy(own_ref.at[pl.ds(part * 8, 8)], held, sem)
    copy.start()
    copy.wait()

    for step in range(0, held.shape[2], BLK):
        columns = slice(step, step + BLK)
        rows = [held[j, :, columns].astype(jnp.float32) for j in range(8)]
        pairs = [(rows[j], sign * rows[j + 4]) for j in range(4)]
        mine = pair_sums(pair_sums([low + high for low, high in pairs], 2), 1)
        theirs = pair_sums(pair_sums([low - high for low, high in pairs], 2), 1)
        for j in range(4):
            mine_ref[j, :, columns] = mine[j]
            send_ref[j, :, columns] = bf16(theirs[j])


def own_sums(own, part):
    width = own.shape[2]
    return pl.pallas_call(
        functools.partial(own_kernel, part),
        out_shape=[
            jax.ShapeDtypeStruct((4, ROWS, width), jnp.float32),
            jax.ShapeDtypeStruct((4, ROWS, width), jnp.bfloat16),
        ],
        in_specs=[pl.BlockSpec(memory_space=pl.ANY)],
        out_specs=whole(2),
        scratch_shapes=[pltpu.VMEM((8, ROWS, width), jnp.bfloat16), pltpu.SemaphoreType.DMA],
        compiler_params=params(),
        cost_estimate=cost(20 * own.size, 3 * own.size),
        name="own_sums",
    )(own)


def last_columns(sign, mine_ref, other_ref, columns):
    scale = 16.0 / math.sqrt(8192.0)
    parts = []
    for j in range(4):
        mine, theirs = mine_ref[j, :, columns], other_ref[j, :, columns].astype(jnp.float32)
        parts.append(bf16((mine + theirs) * scale))
        parts.append(bf16((mine - theirs) * (scale * sign)))
    return jnp.concatenate(parts, axis=0)


def last_kernel(part, mine_ref, other_ref, *refs):
    ffn_ref, heads_ref, ffn_held, heads_held, sems = refs[-5:]
    sign = core_sign()
    copies = []
    for at in range(2):
        there = pl.ds((2 * at + part) * FFN_WIDTH, FFN_WIDTH)
        copies.append(
            pltpu.make_async_copy(ffn_held.at[at], ffn_ref.at[:, there], sems.at[at])
        )
    for at, (start, count) in enumerate(((part * HALF_Q, HALF_Q), (QPG + part, 1))):
        copies.append(
            pltpu.make_async_copy(
                heads_held.at[:, pl.ds(at * HALF_Q * BLK, count * BLK)],
                heads_ref.at[:, pl.ds(start * BLK, count * BLK)],
                sems.at[2 + at],
            )
        )
    for at in range(2):
        for step in range(0, FFN_WIDTH, 2 * BLK):
            source = slice(at * FFN_WIDTH + step, at * FFN_WIDTH + step + 2 * BLK)
            ffn_held[at, :, step : step + 2 * BLK] = last_columns(
                sign, mine_ref, other_ref, source
            )
        copies[at].start()
    for slot in range(HALF_Q + 1):
        source = slice(2 * FFN_WIDTH + slot * BLK, 2 * FFN_WIDTH + (slot + 1) * BLK)
        heads_held[:, slot * BLK : (slot + 1) * BLK] = last_columns(
            sign, mine_ref, other_ref, source
        )
    for copy in copies[2:]:
        copy.start()
    for copy in copies:
        copy.wait()


def last_mix(mine, other, part, targets=()):
    rows = 8 * ROWS
    width = 4 * FFN_WIDTH
    anywhere = pl.BlockSpec(memory_space=pl.ANY)
    return pl.pallas_call(
        functools.partial(last_kernel, part),
        out_shape=[
            jax.ShapeDtypeStruct((rows, width), jnp.bfloat16),
            jax.ShapeDtypeStruct((rows, 2 * HEADS_WIDTH), jnp.bfloat16),
        ],
        in_specs=whole(2) + [anywhere] * len(targets),
        out_specs=[anywhere] * 2,
        input_output_aliases={2: 0, 3: 1} if targets else {},
        scratch_shapes=[
            pltpu.VMEM((2, rows, FFN_WIDTH), jnp.bfloat16),
            pltpu.VMEM((rows, HEADS_WIDTH), jnp.bfloat16),
            pltpu.SemaphoreType.DMA((4,)),
        ],
        compiler_params=params(),
        cost_estimate=cost(20 * rows * width, 3 * rows * width),
        name="last_mix",
    )(mine, other, *targets)


def order_kernel(order_ref, *refs):
    in_refs, (out_ref, slot_ref) = refs[:4], refs[4:]
    owner = lax.axis_index("xl") * 4 + lax.axis_index("y")
    side, z = side_index(), lax.axis_index("z")
    for slot in range(FFB):
        slot_ref[order_ref[owner, slot]] = slot
    groups = in_refs[0].shape[1] // 16
    for r in range(4):
        there = side ^ r
        for place, s in enumerate(SHIFTS):
            shard = (there >> 1) * 2 * DEEP + ((z - s) & (DEEP - 1)) * 2 + (there & 1)
            for group in range(groups):
                at = shard * groups + group
                row = slot_ref[at >> 3] * BLK + (at & 7) * 16
                out_ref[pl.ds(pl.multiple_of(row, 16), 16), :] = in_refs[r][
                    place, group * 16 : (group + 1) * 16, :
                ]


def order_rows(ffn_order, pieces):
    count, rows, width = pieces[0].shape
    return pl.pallas_call(
        order_kernel,
        out_shape=jax.ShapeDtypeStruct((4 * count * rows, width), jnp.bfloat16),
        in_specs=[pl.BlockSpec(memory_space=pltpu.SMEM)] + whole(4),
        out_specs=whole(1)[0],
        scratch_shapes=[pltpu.SMEM((FFB,), jnp.int32)],
        compiler_params=params(),
        cost_estimate=cost(4 * count * rows * width, 16 * count * rows * width),
        name="order_rows",
    )(ffn_order, *pieces)


def exchange(pieces, axes):
    return lax.all_to_all(pieces, axes, split_axis=0, concat_axis=0, tiled=True)


def exchange_apart(go, pieces, axes):
    return lax.cond(go, lambda part: exchange(part, axes), jnp.zeros_like, pieces)


def exchange_z(pieces):
    got = list(pieces)
    for at, s in enumerate(SHIFTS):
        if s:
            got[at] = lax.ppermute(pieces[at], "z", [(i, (i + s) % DEEP) for i in range(DEEP)])
    return got


def exchange_side(pieces, sides):
    got = list(pieces)
    for r in sides:
        got[r] = lax.ppermute(pieces[r], ("xh", "core"), [(i, i ^ r) for i in range(4)])
    return got


def exchange_core(got):
    return lax.ppermute(got, "core", [(0, 1), (1, 0)])


def tie(*arrays):
    return lax.optimization_barrier(arrays)


def per_device(
    q_weight,
    k_weight,
    v_weight,
    gate_weight,
    up_weight,
    down_weight,
    attn_gain,
    ffn_gain,
    head_order,
    ffn_order,
):
    shards = math.prod(lax.axis_size(name) for name in FSDP)
    go = lax.axis_index("z") >= 0
    gates = exchange(pick(ffn_order, ffn_gain, gate_weight), PLANE)
    heads = (head_order, attn_gain, q_weight, k_weight, v_weight)
    rest = pick(ffn_order, ffn_gain, up_weight, heads)
    shifted = exchange_z(rotate_down(down_weight, shards))
    rest, gates = tie(rest, gates)
    rest, *shifted = tie(exchange_apart(go, rest, PLANE), *shifted)
    mixed = exchange(first_mix(gates, rest), DEPTH)
    moved = exchange_side(repack(shifted), (2, 3, 1))
    merged_down = order_rows(ffn_order, moved)
    mixed, merged_down = tie(mixed, merged_down)
    mine, send = own_sums(mixed, 0)
    other = exchange_core(send)
    mixed, mine = tie(mixed, mine)
    mine_next, send = own_sums(mixed, 1)
    other_next = exchange_core(send)
    merged = last_mix(mine, other, 0)
    merged_ffn, merged_attn = last_mix(mine_next, other_next, 1, merged)
    return (merged_attn, merged_ffn, merged_down)


def solution(mesh):
    split = Mesh(mesh.devices.reshape(2, 8, 2, 2, 4), ("xh", "z", "core", "xl", "y"))
    rows = TP + FSDP
    placed = (P(rows, None),) * 6 + (P(rows),) * 2 + (P(), P())
    return jax.shard_map(
        per_device,
        mesh=split,
        in_specs=placed,
        out_specs=(P(FSDP, TP), P(FSDP, TP), P(TP, FSDP)),
        check_vma=False,
    )
```

```python
import functools
import math

import jax
import jax.numpy as jnp
import numpy as np
from jax import lax
from jax.experimental import pallas as pl
from jax.experimental.pallas import tpu as pltpu
from jax.sharding import Mesh
from jax.sharding import PartitionSpec as P

BLK = 128
QPG = 8
FFB = 28
HALF_Q = QPG // 2
HALF_F = FFB // 2
ROWS = 32
PIECES = 16
DEEP = 8
SHIFTS = (0, 1, 7, 3, 5, 2, 6, 4)
FFN_WIDTH = HALF_F * BLK
HEADS_WIDTH = (HALF_Q + 1) * BLK
VMEM_LIMIT = 16 * 1024 * 1024
VMEM_MOST = 56 * 1024 * 1024
PLANE = ("xh", "xl", "y")
DEPTH = ("xh", "z")
FSDP = ("xh", "z", "core")
TP = ("xl", "y")


def signs(order):
    index = np.arange(order)
    common = index[:, None] & index[None, :]
    parity = np.zeros((order, order), np.int64)
    while common.any():
        parity ^= common & 1
        common = common >> 1
    return (1 - 2 * parity).astype(np.float32)


def bf16(values):
    return values.astype(jnp.bfloat16)


def params(limit=VMEM_LIMIT):
    return pltpu.CompilerParams(vmem_limit_bytes=limit)


def cost(flops, moved):
    return pl.CostEstimate(flops=int(flops), bytes_accessed=int(moved), transcendentals=0)


def side_index():
    return lax.axis_index("xh") * 2 + lax.axis_index("core")


def whole(count):
    return [pl.BlockSpec(memory_space=pltpu.VMEM)] * count


def pair_sums(values, span):
    out = list(values)
    for i in range(len(values)):
        if not i & span:
            out[i] = values[i] + values[i | span]
            out[i | span] = values[i] - values[i | span]
    return out


def down_kernel(weight_ref, sign_ref, *refs):
    out_refs, held_ref = refs[:DEEP], refs[DEEP]
    sign = sign_ref[...]
    groups = weight_ref.shape[1] // BLK
    side, z = side_index(), lax.axis_index("z")

    @pl.loop(0, weight_ref.shape[0] // 16)
    def _(step):
        rows = pl.ds(pl.multiple_of(step * 16, 16), 16)
        tall = jnp.concatenate(
            [weight_ref[rows, a * BLK : (a + 1) * BLK] for a in range(groups)], axis=0
        )
        half = jnp.dot(tall, sign, preferred_element_type=jnp.float32)
        half = bf16(half * (1.0 / math.sqrt(BLK))).astype(jnp.float32)
        parts = [half[a * 16 : (a + 1) * 16] for a in range(groups)]
        span = 1
        while span < groups:
            parts = pair_sums(parts, span)
            span *= 2
        for a in range(groups):
            held_ref[a] = bf16(parts[a] * (1.0 / math.sqrt(groups)))
        for at, s in enumerate(SHIFTS):
            for r in range(4):
                there = side ^ r
                shard = (there >> 1) * 2 * DEEP + ((z + s) & (DEEP - 1)) * 2 + (there & 1)
                for a in range(2):
                    out_refs[at][r, rows, a * BLK : (a + 1) * BLK] = held_ref[shard * 2 + a]


def rotate_down(weight, shards):
    rows, width = weight.shape
    groups = width // BLK
    return pl.pallas_call(
        down_kernel,
        out_shape=[jax.ShapeDtypeStruct((4, rows, width // shards), jnp.bfloat16)] * DEEP,
        in_specs=whole(2),
        out_specs=whole(DEEP),
        scratch_shapes=[pltpu.VMEM((groups, 16, BLK), jnp.bfloat16)],
        compiler_params=params(),
        cost_estimate=cost(2 * rows * width * BLK * 4, 4 * rows * width),
        name="down_rotate",
    )(weight, jnp.asarray(signs(BLK), jnp.bfloat16))


def repack_kernel(*refs):
    in_refs, out_refs = refs[:DEEP], refs[DEEP:]
    for r in range(4):
        for s in range(DEEP):
            out_refs[r][s] = in_refs[s][r]


def repack(pieces):
    _, rows, width = pieces[0].shape
    return pl.pallas_call(
        repack_kernel,
        out_shape=[jax.ShapeDtypeStruct((DEEP, rows, width), jnp.bfloat16)] * 4,
        in_specs=whole(DEEP),
        out_specs=whole(4),
        compiler_params=params(),
        cost_estimate=cost(4 * DEEP * rows * width, 16 * DEEP * rows * width),
        name="repack_down",
    )(*pieces)


def spread(gain_ref):
    row = lax.broadcasted_iota(jnp.int32, (ROWS, BLK), 0)
    spread_gain = jnp.zeros((ROWS, BLK), jnp.float32)
    for i in range(ROWS):
        spread_gain = jnp.where(row == i, gain_ref[i], spread_gain)
    return spread_gain


def scaled(ref, block, gain):
    columns = pl.ds(pl.multiple_of(block * BLK, BLK), BLK)
    return bf16(ref[:, columns].astype(jnp.float32) * gain)


def pick_kernel(with_heads, order_ref, ffn_gain_ref, ffn_ref, *refs):
    out_ref = refs[-1]
    ffn_gain = spread(ffn_gain_ref)
    if with_heads:
        heads_ref, attn_gain_ref, q_ref, k_ref, v_ref = refs[:-1]
        attn_gain = spread(attn_gain_ref)
    each = out_ref.shape[0]
    for j in range(each):
        owner, half = j, pl.program_id(0)
        for slot in range(HALF_F):
            block = owner * FFB + order_ref[owner, half * HALF_F + slot]
            out_ref[j, :, slot * BLK : (slot + 1) * BLK] = scaled(ffn_ref, block, ffn_gain)
        if with_heads:
            for slot in range(HALF_Q):
                head = owner * QPG + heads_ref[owner, half * HALF_Q + slot]
                columns = slice(FFN_WIDTH + slot * BLK, FFN_WIDTH + (slot + 1) * BLK)
                out_ref[j, :, columns] = scaled(q_ref, head, attn_gain)
            out_ref[j, :, FFN_WIDTH + HALF_Q * BLK :] = jnp.where(
                half == 1, scaled(v_ref, owner, attn_gain), scaled(k_ref, owner, attn_gain)
            )


def pick(order, gain, weight, heads=()):
    each = 8
    width = FFN_WIDTH + (HEADS_WIDTH if heads else 0)
    small = pl.BlockSpec(memory_space=pltpu.SMEM)
    in_specs = [
        small if array.size < 1024 else pl.BlockSpec(array.shape, lambda i: (0, 0))
        for array in (order, gain, weight, *heads)
    ]
    return pl.pallas_call(
        functools.partial(pick_kernel, bool(heads)),
        grid=(PIECES // each,),
        out_shape=jax.ShapeDtypeStruct((PIECES, ROWS, width), jnp.bfloat16),
        in_specs=in_specs,
        out_specs=pl.BlockSpec((each, ROWS, width), lambda i: (i, 0, 0)),
        compiler_params=params(VMEM_MOST),
        cost_estimate=cost(PIECES * ROWS * width * 400, 4 * PIECES * ROWS * width),
        name="pick_columns",
    )(order, gain, weight, *heads)


def first_kernel(
    groups, matrix_ref, gates_ref, rest_ref, out_ref, held, in_held, out_held, sem, in_sems, out_sems
):
    in_copies, out_copies = [], []
    for at, (array, start, width, begin) in enumerate(groups):
        source = (gates_ref, rest_ref)[array].at[:, :, pl.ds(start, width)]
        there = pl.ds(begin, width)
        in_copies.append(
            pltpu.make_async_copy(source, in_held.at[:, :, there], in_sems.at[at])
        )
        out_copies.append(
            pltpu.make_async_copy(
                out_held.at[:, :, there], out_ref.at[:, :, there], out_sems.at[at]
            )
        )
    whole_matrix = pltpu.make_async_copy(matrix_ref, held, sem)
    whole_matrix.start()
    for copy in in_copies:
        copy.start()
    whole_matrix.wait()
    matrix = held[...]
    for at, (_, _, width, begin) in enumerate(groups):
        in_copies[at].wait()
        for start in range(begin, begin + width, 2 * BLK):
            stop = min(start + 2 * BLK, begin + width)
            sides = [
                jnp.dot(
                    matrix,
                    in_held[side * 8 : side * 8 + 8, :, start:stop].reshape(8 * ROWS, -1),
                    preferred_element_type=jnp.float32,
                )
                for side in range(2)
            ]
            for which, mixed in enumerate((sides[0] + sides[1], sides[0] - sides[1])):
                mixed = bf16(mixed).reshape(8, ROWS, -1)
                for group in range(8):
                    out_held[2 * group + which, :, start:stop] = mixed[group]
        out_copies[at].start()
    for copy in out_copies:
        copy.wait()


def first_mix(gates, rest):
    rows = 8 * ROWS
    width = gates.shape[2] + rest.shape[2]
    groups = []
    for array, blocks in ((0, 4), (0, 10), (1, 10), (1, 6), (1, 3)):
        begin = sum(group[2] for group in groups)
        start = begin - array * gates.shape[2]
        groups.append((array, start, blocks * BLK, begin))
    assert sum(group[2] for group in groups) == width
    held = pltpu.VMEM((PIECES, ROWS, width), jnp.bfloat16)
    sems = pltpu.SemaphoreType.DMA((len(groups),))
    return pl.pallas_call(
        functools.partial(first_kernel, groups),
        out_shape=jax.ShapeDtypeStruct((PIECES, ROWS, width), jnp.bfloat16),
        in_specs=[pl.BlockSpec(memory_space=pl.ANY)] * 3,
        out_specs=pl.BlockSpec(memory_space=pl.ANY),
        scratch_shapes=[
            pltpu.VMEM((rows, rows), jnp.bfloat16),
            held,
            held,
            pltpu.SemaphoreType.DMA,
            sems,
            sems,
        ],
        compiler_params=params(VMEM_MOST),
        cost_estimate=cost(4 * rows * rows * width, 8 * rows * width),
        name="first_mix",
    )(jnp.asarray(signs(rows) / 16.0, jnp.bfloat16), gates, rest)


def core_sign():
    return (1 - 2 * lax.axis_index("core")).astype(jnp.float32)


def own_kernel(part, own_ref, mine_ref, send_ref, held, sems):
    sign = core_sign()
    third = held.shape[2] // 3
    copies = []
    for at in range(3):
        there = pl.ds(at * third, third)
        source = own_ref.at[pl.ds(part * 8, 8), :, there]
        copies.append(pltpu.make_async_copy(source, held.at[:, :, there], sems.at[at]))
    for copy in copies:
        copy.start()

    for step in range(0, held.shape[2], BLK):
        if step % third == 0:
            copies[step // third].wait()
        columns = slice(step, step + BLK)
        rows = [held[j, :, columns].astype(jnp.float32) for j in range(8)]
        pairs = [(rows[j], sign * rows[j + 4]) for j in range(4)]
        mine = pair_sums(pair_sums([low + high for low, high in pairs], 2), 1)
        theirs = pair_sums(pair_sums([low - high for low, high in pairs], 2), 1)
        for j in range(4):
            mine_ref[j, :, columns] = mine[j]
            send_ref[j, :, columns] = bf16(theirs[j])


def own_sums(own, part):
    width = own.shape[2]
    return pl.pallas_call(
        functools.partial(own_kernel, part),
        out_shape=[
            jax.ShapeDtypeStruct((4, ROWS, width), jnp.float32),
            jax.ShapeDtypeStruct((4, ROWS, width), jnp.bfloat16),
        ],
        in_specs=[pl.BlockSpec(memory_space=pl.ANY)],
        out_specs=whole(2),
        scratch_shapes=[pltpu.VMEM((8, ROWS, width), jnp.bfloat16), pltpu.SemaphoreType.DMA((3,))],
        compiler_params=params(),
        cost_estimate=cost(20 * own.size, 3 * own.size),
        name="own_sums",
    )(own)


def last_columns(sign, mine_ref, other_ref, columns):
    scale = 16.0 / math.sqrt(8192.0)
    parts = []
    for j in range(4):
        mine, theirs = mine_ref[j, :, columns], other_ref[j, :, columns].astype(jnp.float32)
        parts.append(bf16((mine + theirs) * scale))
        parts.append(bf16((mine - theirs) * (scale * sign)))
    return jnp.concatenate(parts, axis=0)


def last_kernel(part, mine_ref, other_ref, *refs):
    ffn_ref, heads_ref, ffn_held, heads_held, sems = refs[-5:]
    sign = core_sign()
    copies = []
    for at in range(2):
        there = pl.ds((2 * at + part) * FFN_WIDTH, FFN_WIDTH)
        copies.append(
            pltpu.make_async_copy(ffn_held.at[at], ffn_ref.at[:, there], sems.at[at])
        )
    for at, (start, count) in enumerate(((part * HALF_Q, HALF_Q), (QPG + part, 1))):
        copies.append(
            pltpu.make_async_copy(
                heads_held.at[:, pl.ds(at * HALF_Q * BLK, count * BLK)],
                heads_ref.at[:, pl.ds(start * BLK, count * BLK)],
                sems.at[2 + at],
            )
        )
    for at in range(2):
        for step in range(0, FFN_WIDTH, 2 * BLK):
            source = slice(at * FFN_WIDTH + step, at * FFN_WIDTH + step + 2 * BLK)
            ffn_held[at, :, step : step + 2 * BLK] = last_columns(
                sign, mine_ref, other_ref, source
            )
        copies[at].start()
    for slot in range(HALF_Q + 1):
        source = slice(2 * FFN_WIDTH + slot * BLK, 2 * FFN_WIDTH + (slot + 1) * BLK)
        heads_held[:, slot * BLK : (slot + 1) * BLK] = last_columns(
            sign, mine_ref, other_ref, source
        )
    for copy in copies[2:]:
        copy.start()
    for copy in copies:
        copy.wait()


def last_mix(mine, other, part, targets=()):
    rows = 8 * ROWS
    width = 4 * FFN_WIDTH
    anywhere = pl.BlockSpec(memory_space=pl.ANY)
    return pl.pallas_call(
        functools.partial(last_kernel, part),
        out_shape=[
            jax.ShapeDtypeStruct((rows, width), jnp.bfloat16),
            jax.ShapeDtypeStruct((rows, 2 * HEADS_WIDTH), jnp.bfloat16),
        ],
        in_specs=whole(2) + [anywhere] * len(targets),
        out_specs=[anywhere] * 2,
        input_output_aliases={2: 0, 3: 1} if targets else {},
        scratch_shapes=[
            pltpu.VMEM((2, rows, FFN_WIDTH), jnp.bfloat16),
            pltpu.VMEM((rows, HEADS_WIDTH), jnp.bfloat16),
            pltpu.SemaphoreType.DMA((4,)),
        ],
        compiler_params=params(),
        cost_estimate=cost(20 * rows * width, 3 * rows * width),
        name="last_mix",
    )(mine, other, *targets)


def order_kernel(order_ref, *refs):
    in_refs, (out_ref, slot_ref) = refs[:4], refs[4:]
    owner = lax.axis_index("xl") * 4 + lax.axis_index("y")
    side, z = side_index(), lax.axis_index("z")
    for slot in range(FFB):
        slot_ref[order_ref[owner, slot]] = slot
    groups = in_refs[0].shape[1] // 16
    for r in range(4):
        there = side ^ r
        for place, s in enumerate(SHIFTS):
            shard = (there >> 1) * 2 * DEEP + ((z - s) & (DEEP - 1)) * 2 + (there & 1)
            for group in range(groups):
                at = shard * groups + group
                row = slot_ref[at >> 3] * BLK + (at & 7) * 16
                out_ref[pl.ds(pl.multiple_of(row, 16), 16), :] = in_refs[r][
                    place, group * 16 : (group + 1) * 16, :
                ]


def order_rows(ffn_order, pieces):
    count, rows, width = pieces[0].shape
    return pl.pallas_call(
        order_kernel,
        out_shape=jax.ShapeDtypeStruct((4 * count * rows, width), jnp.bfloat16),
        in_specs=[pl.BlockSpec(memory_space=pltpu.SMEM)] + whole(4),
        out_specs=whole(1)[0],
        scratch_shapes=[pltpu.SMEM((FFB,), jnp.int32)],
        compiler_params=params(),
        cost_estimate=cost(4 * count * rows * width, 16 * count * rows * width),
        name="order_rows",
    )(ffn_order, *pieces)


def exchange(pieces, axes):
    return lax.all_to_all(pieces, axes, split_axis=0, concat_axis=0, tiled=True)


def exchange_apart(go, pieces, axes):
    return lax.cond(go, lambda part: exchange(part, axes), jnp.zeros_like, pieces)


def exchange_z(pieces):
    got = list(pieces)
    for at, s in enumerate(SHIFTS):
        if s:
            got[at] = lax.ppermute(pieces[at], "z", [(i, (i + s) % DEEP) for i in range(DEEP)])
    return got


def exchange_side(pieces, sides):
    got = list(pieces)
    for r in sides:
        got[r] = lax.ppermute(pieces[r], ("xh", "core"), [(i, i ^ r) for i in range(4)])
    return got


def exchange_core(got):
    return lax.ppermute(got, "core", [(0, 1), (1, 0)])


def tie(*arrays):
    return lax.optimization_barrier(arrays)


def per_device(
    q_weight,
    k_weight,
    v_weight,
    gate_weight,
    up_weight,
    down_weight,
    attn_gain,
    ffn_gain,
    head_order,
    ffn_order,
):
    shards = math.prod(lax.axis_size(name) for name in FSDP)
    go = lax.axis_index("z") >= 0
    gates = exchange(pick(ffn_order, ffn_gain, gate_weight), PLANE)
    heads = (head_order, attn_gain, q_weight, k_weight, v_weight)
    rest = pick(ffn_order, ffn_gain, up_weight, heads)
    shifted = exchange_z(rotate_down(down_weight, shards))
    rest, gates = tie(rest, gates)
    rest, *shifted = tie(exchange_apart(go, rest, PLANE), *shifted)
    mixed = exchange(first_mix(gates, rest), DEPTH)
    moved = exchange_side(repack(shifted), (2, 3, 1))
    merged_down = order_rows(ffn_order, moved)
    mixed, merged_down = tie(mixed, merged_down)
    mine, send = own_sums(mixed, 0)
    other = exchange_core(send)
    mixed, mine = tie(mixed, mine)
    mine_next, send = own_sums(mixed, 1)
    other_next = exchange_core(send)
    merged = last_mix(mine, other, 0)
    merged_ffn, merged_attn = last_mix(mine_next, other_next, 1, merged)
    return (merged_attn, merged_ffn, merged_down)


def solution(mesh):
    split = Mesh(mesh.devices.reshape(2, 8, 2, 2, 4), ("xh", "z", "core", "xl", "y"))
    rows = TP + FSDP
    placed = (P(rows, None),) * 6 + (P(rows),) * 2 + (P(), P())
    return jax.shard_map(
        per_device,
        mesh=split,
        in_specs=placed,
        out_specs=(P(FSDP, TP), P(FSDP, TP), P(TP, FSDP)),
        check_vma=False,
    )
```

```python
import functools
import math

import jax
import jax.numpy as jnp
import numpy as np
from jax import lax
from jax.experimental import pallas as pl
from jax.experimental.pallas import tpu as pltpu
from jax.sharding import Mesh
from jax.sharding import PartitionSpec as P

BLK = 128
QPG = 8
FFB = 28
HALF_Q = QPG // 2
HALF_F = FFB // 2
ROWS = 32
PIECES = 16
DEEP = 8
SHIFTS = (0, 1, 7, 2, 6, 3, 5, 4)
FFN_WIDTH = HALF_F * BLK
HEADS_WIDTH = (HALF_Q + 1) * BLK
VMEM_LIMIT = 16 * 1024 * 1024
VMEM_MOST = 56 * 1024 * 1024
PLANE = ("xh", "xl", "y")
DEPTH = ("xh", "z")
FSDP = ("xh", "z", "core")
TP = ("xl", "y")


def signs(order):
    index = np.arange(order)
    common = index[:, None] & index[None, :]
    parity = np.zeros((order, order), np.int64)
    while common.any():
        parity ^= common & 1
        common = common >> 1
    return (1 - 2 * parity).astype(np.float32)


def bf16(values):
    return values.astype(jnp.bfloat16)


def params(limit=VMEM_LIMIT):
    return pltpu.CompilerParams(vmem_limit_bytes=limit)


def cost(flops, moved):
    return pl.CostEstimate(flops=int(flops), bytes_accessed=int(moved), transcendentals=0)


def side_index():
    return lax.axis_index("xh") * 2 + lax.axis_index("core")


def whole(count):
    return [pl.BlockSpec(memory_space=pltpu.VMEM)] * count


def pair_sums(values, span):
    out = list(values)
    for i in range(len(values)):
        if not i & span:
            out[i] = values[i] + values[i | span]
            out[i | span] = values[i] - values[i | span]
    return out


def down_kernel(weight_ref, sign_ref, *refs):
    out_refs, held_ref = refs[:DEEP], refs[DEEP]
    sign = sign_ref[...]
    groups = weight_ref.shape[1] // BLK
    side, z = side_index(), lax.axis_index("z")

    @pl.loop(0, weight_ref.shape[0] // 16)
    def _(step):
        rows = pl.ds(pl.multiple_of(step * 16, 16), 16)
        tall = jnp.concatenate(
            [weight_ref[rows, a * BLK : (a + 1) * BLK] for a in range(groups)], axis=0
        )
        half = jnp.dot(tall, sign, preferred_element_type=jnp.float32)
        half = bf16(half * (1.0 / math.sqrt(BLK))).astype(jnp.float32)
        parts = [half[a * 16 : (a + 1) * 16] for a in range(groups)]
        span = 1
        while span < groups:
            parts = pair_sums(parts, span)
            span *= 2
        for a in range(groups):
            held_ref[a] = bf16(parts[a] * (1.0 / math.sqrt(groups)))
        for at, s in enumerate(SHIFTS):
            for r in range(4):
                there = side ^ r
                shard = (there >> 1) * 2 * DEEP + ((z + s) & (DEEP - 1)) * 2 + (there & 1)
                for a in range(2):
                    out_refs[at][r, rows, a * BLK : (a + 1) * BLK] = held_ref[shard * 2 + a]


def rotate_down(weight, shards):
    rows, width = weight.shape
    groups = width // BLK
    return pl.pallas_call(
        down_kernel,
        out_shape=[jax.ShapeDtypeStruct((4, rows, width // shards), jnp.bfloat16)] * DEEP,
        in_specs=whole(2),
        out_specs=whole(DEEP),
        scratch_shapes=[pltpu.VMEM((groups, 16, BLK), jnp.bfloat16)],
        compiler_params=params(),
        cost_estimate=cost(2 * rows * width * BLK * 4, 4 * rows * width),
        name="down_rotate",
    )(weight, jnp.asarray(signs(BLK), jnp.bfloat16))


def repack_kernel(*refs):
    in_refs, out_refs = refs[:DEEP], refs[DEEP:]
    for r in range(4):
        for s in range(DEEP):
            out_refs[r][s] = in_refs[s][r]


def repack(pieces):
    _, rows, width = pieces[0].shape
    return pl.pallas_call(
        repack_kernel,
        out_shape=[jax.ShapeDtypeStruct((DEEP, rows, width), jnp.bfloat16)] * 4,
        in_specs=whole(DEEP),
        out_specs=whole(4),
        compiler_params=params(),
        cost_estimate=cost(4 * DEEP * rows * width, 16 * DEEP * rows * width),
        name="repack_down",
    )(*pieces)


def spread(gain_ref):
    row = lax.broadcasted_iota(jnp.int32, (ROWS, BLK), 0)
    spread_gain = jnp.zeros((ROWS, BLK), jnp.float32)
    for i in range(ROWS):
        spread_gain = jnp.where(row == i, gain_ref[i], spread_gain)
    return spread_gain


def scaled(ref, block, gain):
    columns = pl.ds(pl.multiple_of(block * BLK, BLK), BLK)
    return bf16(ref[:, columns].astype(jnp.float32) * gain)


def pick_kernel(with_heads, order_ref, ffn_gain_ref, ffn_ref, *refs):
    out_ref = refs[-1]
    ffn_gain = spread(ffn_gain_ref)
    if with_heads:
        heads_ref, attn_gain_ref, q_ref, k_ref, v_ref = refs[:-1]
        attn_gain = spread(attn_gain_ref)
    each = out_ref.shape[0]
    for j in range(each):
        owner, half = j, pl.program_id(0)
        for slot in range(HALF_F):
            block = owner * FFB + order_ref[owner, half * HALF_F + slot]
            out_ref[j, :, slot * BLK : (slot + 1) * BLK] = scaled(ffn_ref, block, ffn_gain)
        if with_heads:
            for slot in range(HALF_Q):
                head = owner * QPG + heads_ref[owner, half * HALF_Q + slot]
                columns = slice(FFN_WIDTH + slot * BLK, FFN_WIDTH + (slot + 1) * BLK)
                out_ref[j, :, columns] = scaled(q_ref, head, attn_gain)
            out_ref[j, :, FFN_WIDTH + HALF_Q * BLK :] = jnp.where(
                half == 1, scaled(v_ref, owner, attn_gain), scaled(k_ref, owner, attn_gain)
            )


def pick(order, gain, weight, heads=()):
    each = 8
    width = FFN_WIDTH + (HEADS_WIDTH if heads else 0)
    small = pl.BlockSpec(memory_space=pltpu.SMEM)
    in_specs = [
        small if array.size < 1024 else pl.BlockSpec(array.shape, lambda i: (0, 0))
        for array in (order, gain, weight, *heads)
    ]
    return pl.pallas_call(
        functools.partial(pick_kernel, bool(heads)),
        grid=(PIECES // each,),
        out_shape=jax.ShapeDtypeStruct((PIECES, ROWS, width), jnp.bfloat16),
        in_specs=in_specs,
        out_specs=pl.BlockSpec((each, ROWS, width), lambda i: (i, 0, 0)),
        compiler_params=params(VMEM_MOST),
        cost_estimate=cost(PIECES * ROWS * width * 400, 4 * PIECES * ROWS * width),
        name="pick_columns",
    )(order, gain, weight, *heads)


def first_kernel(
    groups, matrix_ref, gates_ref, rest_ref, out_ref, held, in_held, out_held, sem, in_sems, out_sems
):
    in_copies, out_copies = [], []
    for at, (array, start, width, begin) in enumerate(groups):
        there = pl.ds(begin, width)
        if array:
            source = rest_ref.at[:, :, pl.ds(start, width)]
            in_copies.append(
                pltpu.make_async_copy(source, in_held.at[:, :, pl.ds(start, width)], in_sems.at[at])
            )
        else:
            in_copies.append(None)
        out_copies.append(
            pltpu.make_async_copy(
                out_held.at[:, :, there], out_ref.at[:, :, there], out_sems.at[at]
            )
        )
    whole_matrix = pltpu.make_async_copy(matrix_ref, held, sem)
    whole_matrix.start()
    for copy in in_copies:
        if copy is not None:
            copy.start()
    whole_matrix.wait()
    matrix = held[...]
    for at, (array, first, width, begin) in enumerate(groups):
        if array:
            in_copies[at].wait()
        tall_ref = in_held if array else gates_ref
        for start in range(begin, begin + width, 2 * BLK):
            stop = min(start + 2 * BLK, begin + width)
            columns = slice(start - begin + first, stop - begin + first)
            sides = [
                jnp.dot(
                    matrix,
                    tall_ref[side * 8 : side * 8 + 8, :, columns].reshape(8 * ROWS, -1),
                    preferred_element_type=jnp.float32,
                )
                for side in range(2)
            ]
            for which, mixed in enumerate((sides[0] + sides[1], sides[0] - sides[1])):
                mixed = bf16(mixed).reshape(8, ROWS, -1)
                for group in range(8):
                    out_held[2 * group + which, :, start:stop] = mixed[group]
        out_copies[at].start()
    for copy in out_copies:
        copy.wait()


def first_mix(gates, rest):
    rows = 8 * ROWS
    width = gates.shape[2] + rest.shape[2]
    groups = []
    for array, blocks in ((0, 4), (0, 10), (1, 10), (1, 6), (1, 3)):
        begin = sum(group[2] for group in groups)
        start = begin - array * gates.shape[2]
        groups.append((array, start, blocks * BLK, begin))
    assert sum(group[2] for group in groups) == width
    held = pltpu.VMEM((PIECES, ROWS, width), jnp.bfloat16)
    sems = pltpu.SemaphoreType.DMA((len(groups),))
    return pl.pallas_call(
        functools.partial(first_kernel, groups),
        out_shape=jax.ShapeDtypeStruct((PIECES, ROWS, width), jnp.bfloat16),
        in_specs=[
            pl.BlockSpec(memory_space=pl.ANY),
            *whole(1),
            pl.BlockSpec(memory_space=pl.ANY),
        ],
        out_specs=pl.BlockSpec(memory_space=pl.ANY),
        scratch_shapes=[
            pltpu.VMEM((rows, rows), jnp.bfloat16),
            pltpu.VMEM(rest.shape, jnp.bfloat16),
            held,
            pltpu.SemaphoreType.DMA,
            sems,
            sems,
        ],
        compiler_params=params(),
        cost_estimate=cost(4 * rows * rows * width, 8 * rows * width),
        name="first_mix",
    )(jnp.asarray(signs(rows) / 16.0, jnp.bfloat16), gates, rest)


def core_sign():
    return (1 - 2 * lax.axis_index("core")).astype(jnp.float32)


def own_kernel(part, own_ref, mine_ref, send_ref, held, sems):
    sign = core_sign()
    third = held.shape[2] // 3
    copies = []
    for at in range(3):
        there = pl.ds(at * third, third)
        source = own_ref.at[pl.ds(part * 8, 8), :, there]
        copies.append(pltpu.make_async_copy(source, held.at[:, :, there], sems.at[at]))
    for copy in copies:
        copy.start()

    for step in range(0, held.shape[2], BLK):
        if step % third == 0:
            copies[step // third].wait()
        columns = slice(step, step + BLK)
        rows = [held[j, :, columns].astype(jnp.float32) for j in range(8)]
        pairs = [(rows[j], sign * rows[j + 4]) for j in range(4)]
        mine = pair_sums(pair_sums([low + high for low, high in pairs], 2), 1)
        theirs = pair_sums(pair_sums([low - high for low, high in pairs], 2), 1)
        for j in range(4):
            mine_ref[j, :, columns] = mine[j]
            send_ref[j, :, columns] = bf16(theirs[j])


def own_sums(own, part):
    width = own.shape[2]
    return pl.pallas_call(
        functools.partial(own_kernel, part),
        out_shape=[
            jax.ShapeDtypeStruct((4, ROWS, width), jnp.float32),
            jax.ShapeDtypeStruct((4, ROWS, width), jnp.bfloat16),
        ],
        in_specs=[pl.BlockSpec(memory_space=pl.ANY)],
        out_specs=whole(2),
        scratch_shapes=[pltpu.VMEM((8, ROWS, width), jnp.bfloat16), pltpu.SemaphoreType.DMA((3,))],
        compiler_params=params(),
        cost_estimate=cost(20 * own.size, 3 * own.size),
        name="own_sums",
    )(own)


def last_columns(sign, mine_ref, other_ref, columns):
    scale = 16.0 / math.sqrt(8192.0)
    parts = []
    for j in range(4):
        mine, theirs = mine_ref[j, :, columns], other_ref[j, :, columns].astype(jnp.float32)
        parts.append(bf16((mine + theirs) * scale))
        parts.append(bf16((mine - theirs) * (scale * sign)))
    return jnp.concatenate(parts, axis=0)


def last_kernel(part, mine_ref, other_ref, *refs):
    ffn_ref, heads_ref, ffn_held, heads_held, sems = refs[-5:]
    sign = core_sign()
    copies = []
    for at in range(2):
        there = pl.ds((2 * at + part) * FFN_WIDTH, FFN_WIDTH)
        copies.append(
            pltpu.make_async_copy(ffn_held.at[at], ffn_ref.at[:, there], sems.at[at])
        )
    for at, (start, count) in enumerate(((part * HALF_Q, HALF_Q), (QPG + part, 1))):
        copies.append(
            pltpu.make_async_copy(
                heads_held.at[:, pl.ds(at * HALF_Q * BLK, count * BLK)],
                heads_ref.at[:, pl.ds(start * BLK, count * BLK)],
                sems.at[2 + at],
            )
        )
    for at in range(2):
        for step in range(0, FFN_WIDTH, 2 * BLK):
            source = slice(at * FFN_WIDTH + step, at * FFN_WIDTH + step + 2 * BLK)
            ffn_held[at, :, step : step + 2 * BLK] = last_columns(
                sign, mine_ref, other_ref, source
            )
        copies[at].start()
    for slot in range(HALF_Q + 1):
        source = slice(2 * FFN_WIDTH + slot * BLK, 2 * FFN_WIDTH + (slot + 1) * BLK)
        heads_held[:, slot * BLK : (slot + 1) * BLK] = last_columns(
            sign, mine_ref, other_ref, source
        )
    for copy in copies[2:]:
        copy.start()
    for copy in copies:
        copy.wait()


def last_mix(mine, other, part, targets=()):
    rows = 8 * ROWS
    width = 4 * FFN_WIDTH
    anywhere = pl.BlockSpec(memory_space=pl.ANY)
    return pl.pallas_call(
        functools.partial(last_kernel, part),
        out_shape=[
            jax.ShapeDtypeStruct((rows, width), jnp.bfloat16),
            jax.ShapeDtypeStruct((rows, 2 * HEADS_WIDTH), jnp.bfloat16),
        ],
        in_specs=whole(2) + [anywhere] * len(targets),
        out_specs=[anywhere] * 2,
        input_output_aliases={2: 0, 3: 1} if targets else {},
        scratch_shapes=[
            pltpu.VMEM((2, rows, FFN_WIDTH), jnp.bfloat16),
            pltpu.VMEM((rows, HEADS_WIDTH), jnp.bfloat16),
            pltpu.SemaphoreType.DMA((4,)),
        ],
        compiler_params=params(),
        cost_estimate=cost(20 * rows * width, 3 * rows * width),
        name="last_mix",
    )(mine, other, *targets)


def order_kernel(order_ref, *refs):
    in_refs, (out_ref, slot_ref) = refs[:4], refs[4:]
    owner = lax.axis_index("xl") * 4 + lax.axis_index("y")
    side, z = side_index(), lax.axis_index("z")
    for slot in range(FFB):
        slot_ref[order_ref[owner, slot]] = slot
    groups = in_refs[0].shape[1] // 16
    for r in range(4):
        there = side ^ r
        for place, s in enumerate(SHIFTS):
            shard = (there >> 1) * 2 * DEEP + ((z - s) & (DEEP - 1)) * 2 + (there & 1)
            for group in range(groups):
                at = shard * groups + group
                row = slot_ref[at >> 3] * BLK + (at & 7) * 16
                out_ref[pl.ds(pl.multiple_of(row, 16), 16), :] = in_refs[r][
                    place, group * 16 : (group + 1) * 16, :
                ]


def order_rows(ffn_order, pieces):
    count, rows, width = pieces[0].shape
    return pl.pallas_call(
        order_kernel,
        out_shape=jax.ShapeDtypeStruct((4 * count * rows, width), jnp.bfloat16),
        in_specs=[pl.BlockSpec(memory_space=pltpu.SMEM)] + whole(4),
        out_specs=whole(1)[0],
        scratch_shapes=[pltpu.SMEM((FFB,), jnp.int32)],
        compiler_params=params(),
        cost_estimate=cost(4 * count * rows * width, 16 * count * rows * width),
        name="order_rows",
    )(ffn_order, *pieces)


def exchange(pieces, axes):
    return lax.all_to_all(pieces, axes, split_axis=0, concat_axis=0, tiled=True)


def exchange_apart(go, pieces, axes):
    return lax.cond(go, lambda part: exchange(part, axes), jnp.zeros_like, pieces)


def exchange_z(pieces):
    got = list(pieces)
    for at, s in enumerate(SHIFTS):
        if s:
            got[at] = lax.ppermute(pieces[at], "z", [(i, (i + s) % DEEP) for i in range(DEEP)])
    return got


def exchange_side(pieces, sides):
    got = list(pieces)
    for r in sides:
        got[r] = lax.ppermute(pieces[r], ("xh", "core"), [(i, i ^ r) for i in range(4)])
    return got


def exchange_core(got):
    return lax.ppermute(got, "core", [(0, 1), (1, 0)])


def tie(*arrays):
    return lax.optimization_barrier(arrays)


def per_device(
    q_weight,
    k_weight,
    v_weight,
    gate_weight,
    up_weight,
    down_weight,
    attn_gain,
    ffn_gain,
    head_order,
    ffn_order,
):
    shards = math.prod(lax.axis_size(name) for name in FSDP)
    go = lax.axis_index("z") >= 0
    gates = exchange(pick(ffn_order, ffn_gain, gate_weight), PLANE)
    heads = (head_order, attn_gain, q_weight, k_weight, v_weight)
    rest = pick(ffn_order, ffn_gain, up_weight, heads)
    shifted = exchange_z(rotate_down(down_weight, shards))
    rest, gates = tie(rest, gates)
    rest, *shifted = tie(exchange_apart(go, rest, PLANE), *shifted)
    mixed = exchange(first_mix(gates, rest), DEPTH)
    moved = exchange_side(repack(shifted), (2, 3, 1))
    merged_down = order_rows(ffn_order, moved)
    mixed, merged_down = tie(mixed, merged_down)
    mine, send = own_sums(mixed, 0)
    other = exchange_core(send)
    mixed, mine = tie(mixed, mine)
    mine_next, send = own_sums(mixed, 1)
    other_next = exchange_core(send)
    merged = last_mix(mine, other, 0)
    merged_ffn, merged_attn = last_mix(mine_next, other_next, 1, merged)
    return (merged_attn, merged_ffn, merged_down)


def solution(mesh):
    split = Mesh(mesh.devices.reshape(2, 8, 2, 2, 4), ("xh", "z", "core", "xl", "y"))
    rows = TP + FSDP
    placed = (P(rows, None),) * 6 + (P(rows),) * 2 + (P(), P())
    return jax.shard_map(
        per_device,
        mesh=split,
        in_specs=placed,
        out_specs=(P(FSDP, TP), P(FSDP, TP), P(TP, FSDP)),
        check_vma=False,
    )
```
